32 devices in a mesh: grid: 8 (over z, y), rep: 4 (over x, core).
Axes of the slice: x: 2, y: 2, z: 4, core: 2. Of those that a mesh axis runs over, the one named last changes fastest.
Arguments:
- integrals: bfloat16 [16384, 512], P(('grid', 'rep')), may hold values from -6 to 6
- green_occ: bfloat16 [512, 2048], P(None, 'grid'), may hold values from -0.25 to 0.25
- tile_panels: int32 [128, 2], P(('grid', 'rep')), may hold values from 0 to 7, all different within a row; in each aligned block of 4 rows (0 to 3, 4 to 7, ...) at most 2 rows name the same one
- virtual_blocks: bfloat16 [8, 16, 256, 256], P('grid', 'rep'), may hold values from -0.06591797 to 0.06591797
Outputs:
- response_blocks: float32 [8, 128, 256], P('grid', 'rep')
The draws below stay inside these ranges and needn't reach their ends.
Inputs may be any that keep to these rules, and one draw needn't show every extreme that they name: `tile_panels`: each row lists 2 different panels. In each aligned block of 4 rows (the tiles of one device) no panel is listed by more than 2 rows, and some panel is listed by exactly 2 rows.
All inputs are finite; a program needn't handle non-finite values.
Results may differ from the reference program's by a relative error of at most 0.0029.
Values may be sent and summed in bfloat16 or wider, within the bound.
No kernel may reach another device: no remote copies, remote signals or barrier semaphores. Data moves between devices by JAX's collectives and lax.ppermute only.
A program may use at most 128 MiB of HBM per device.

```python
import math
import jax
import jax.numpy as jnp
import numpy as np
from jax import lax

K = 512
W = 256
C = 256
TR = 128
NTD = 4
CAP = 2
NSEL = 2
NB = 16
TILES = 128
LAM = 2048
ROWS = 16384
N_GRID = 8


def steps_of(key, shape, cuts, low, largest):
    def one(position, shards_of):
        steps = jax.random.uniform(jax.random.fold_in(jax.random.fold_in(key, 6), position), (shards_of,), jnp.float32, low / len(cuts), largest / len(cuts))
        return jnp.repeat(jnp.exp(steps), shape[position] // shards_of).reshape((-1,) + (1,) * (len(shape) - position - 1))

    loudness = one(*cuts[0])
    for cut in cuts[1:]:
        loudness = loudness * one(*cut)
    return loudness


def deal_out(rng, own, number, rows, amount, top, limit, lean):
    ranking = jax.random.permutation(rng, amount)
    packed, ordinary = portions_of(amount, rows * top, limit, lean, True), portions_of(amount, rows * top, limit, lean, False)
    places = jnp.arange(amount)

    def named(sizes, rotation):
        used = int((sizes > 0).sum())
        fixed = max(1, used // 4)
        shifted = fixed + (places - fixed + rotation * (used - fixed)) % max(1, amount - fixed)
        return jnp.zeros((amount,), jnp.int32).at[ranking[jnp.where(places < fixed, places, shifted)]].set(jnp.asarray(sizes, jnp.int32))

    sizes = jnp.where(number % 4 == 0, named(packed, number // 4), named(ordinary, number - number // 4 - 1))
    mixed = jax.random.permutation(jax.random.fold_in(own, 3), amount)
    source_of, taker = mixed[0:amount // 2 * 2:2], mixed[1:amount // 2 * 2:2]
    margin = jnp.minimum(sizes[source_of] - 1, limit - sizes[taker]) // 2
    margin = jnp.where((source_of == ranking[0]) | (taker == ranking[0]) | (sizes[taker] == 0), 0, jnp.maximum(margin, 0))
    shifted = jax.random.randint(jax.random.fold_in(own, 4), (amount // 2,), 0, 1 << 20) % (margin + 1)
    sizes = sizes.at[source_of].add(-shifted).at[taker].add(shifted)
    labels = jnp.searchsorted(jnp.cumsum(sizes), jnp.arange(rows * top), side="right").astype(jnp.int32)
    grid = labels.reshape(top, rows).T
    grid = grid[jax.random.permutation(jax.random.fold_in(own, 1), rows)]
    rotation = jax.random.randint(jax.random.fold_in(own, 2), (rows, 1), 0, top)
    return jnp.take_along_axis(grid, (jnp.arange(top)[None, :] + rotation) % top, axis=1)


def portions_of(count, total, reach, skew, full):
    loads = [(1 << 20) // math.isqrt(standing ** skew) + 1 for standing in range(1, count + 1)]
    largest = reach if full else min(reach, max(-(-total // count), total * loads[0] // sum(loads)))
    least = 1 if total - largest >= count - 1 else 0
    counts, spare = [largest] + [least] * (count - 1), total - largest - least * (count - 1)
    while spare > 0:
        free = [i for i in range(1, count) if counts[i] < largest] or [i for i in range(1, count) if counts[i] < reach]
        pool, left = sum([loads[i] for i in free]), spare
        for i in free:
            more = min(reach - counts[i], max(1, left * loads[i] // pool), spare)
            counts[i] = counts[i] + more
            spare = spare - more
    return np.array(counts)


def normal_values(own_key, shape, scale, reach, shards=(), held_as=jnp.bfloat16):
    result = scale * jax.random.normal(own_key, shape, jnp.float32)
    if shards:
        result = result * steps_of(own_key, shape, shards, -0.22, 0.18)
    return jnp.clip(result, -reach, reach).astype(held_as)


def setup_inputs(seed: int = 0) -> dict:
    streams_of = jax.random.split(jax.random.key(seed), 5)
    integrals = normal_values(streams_of[0], (ROWS, K), 1.0, 6.0, ((0, 32),))
    green_occ = normal_values(streams_of[1], (K, LAM), K ** -0.5, 0.25, ((1, 8),))
    tile_panels_keys = jax.random.split(jax.random.fold_in(streams_of[2], 1), TILES // NTD)
    tile_panels_turns = jax.random.permutation(jax.random.fold_in(streams_of[2], 3), TILES // NTD)
    tile_panels = jax.vmap(lambda own, number: deal_out(jax.random.fold_in(streams_of[2], 2), own, number, NTD, N_GRID, NSEL, CAP, 2))(tile_panels_keys, tile_panels_turns).reshape((TILES, NSEL))
    virtual_blocks = normal_values(streams_of[3], (N_GRID, NB, W, C), (1.0 / (W * NSEL * NB) ** 0.5), 0.06591797, ((0, 8), (1, 4)))
    return dict(integrals=integrals, green_occ=green_occ, tile_panels=tile_panels, virtual_blocks=virtual_blocks)


def reference(integrals, green_occ, tile_panels, virtual_blocks):
    grid_count = virtual_blocks.shape[0]
    block_count = virtual_blocks.shape[1]
    tile_count = tile_panels.shape[0]
    panels = green_occ.astype(jnp.float32).reshape(K, grid_count, W)
    tile_stack = integrals.reshape(tile_count, TR, K)

    def accumulate(running, tile_index):
        tile_block = tile_stack[tile_index].astype(jnp.float32)
        chosen = tile_panels[tile_index]
        chosen_panels = jnp.take(panels, chosen, axis=1)
        products = jnp.einsum("tk,ksw->stw", tile_block, chosen_panels, precision=lax.Precision.HIGHEST)
        rounded = lax.optimization_barrier(products.astype(jnp.bfloat16))
        block_index = tile_index % block_count
        running = running.at[chosen, block_index].add(rounded.astype(jnp.float32))
        return running, None

    start_sums = jnp.zeros((grid_count, block_count, TR, W), jnp.float32)
    summed, _ = lax.scan(accumulate, start_sums, jnp.arange(tile_count, dtype=jnp.int32))
    return jnp.einsum("jbtw,jbwc->jtc", summed, virtual_blocks.astype(jnp.float32), precision=lax.Precision.HIGHEST)
```

```python
import functools

import jax
import jax.numpy as jnp
from jax import lax
from jax.experimental import pallas as pl
from jax.experimental.pallas import tpu as pltpu
from jax.sharding import PartitionSpec as P

AXES = ("grid", "rep")
CAP = 2
LABEL_ROWS = 16


def contract_kernel(panel, listed, own, sibling, green, message, chosen):
    tiles, rows, _ = own.shape
    hits = []
    for block, source in enumerate((own, sibling)):
        picks, count = [jnp.int32(0)] * CAP, jnp.int32(0)
        for tile in range(tiles):
            hit = functools.reduce(
                jnp.logical_or, [listed[block, tile, s] == panel[0] for s in range(listed.shape[2])]
            )
            picks = [jnp.where(hit & (count == n), tile, pick) for n, pick in enumerate(picks)]
            count = count + hit.astype(jnp.int32)
        for n, pick in enumerate(picks):
            slot = block * CAP + n
            chosen[slot * rows : (slot + 1) * rows, :] = source[pick]
            hits.append((n < count, block * tiles + pick))
    product = jnp.dot(chosen[...], green[...], preferred_element_type=jnp.float32)
    width = message.shape[1]
    line = lax.broadcasted_iota(jnp.int32, (LABEL_ROWS, width), 0)
    labels = jnp.zeros((LABEL_ROWS, width), jnp.float32)
    for slot, (used, label) in enumerate(hits):
        part = product[slot * rows : (slot + 1) * rows]
        part = jnp.where(used, part, jnp.zeros_like(part))
        message[slot * rows : (slot + 1) * rows, :] = part.astype(message.dtype)
        labels = jnp.where((line == slot) & used, label.astype(jnp.float32), labels)
    message[len(hits) * rows :, :] = labels.astype(message.dtype)


def contract(panel, listed, own, sibling, green):
    tiles, rows, depth = own.shape
    slots, width = 2 * CAP, green.shape[1]
    smem, vmem = pl.BlockSpec(memory_space=pltpu.SMEM), pl.BlockSpec(memory_space=pltpu.VMEM)
    return pl.pallas_call(
        contract_kernel,
        out_shape=jax.ShapeDtypeStruct((slots * rows + LABEL_ROWS, width), jnp.bfloat16),
        in_specs=[smem, smem, vmem, vmem, vmem],
        out_specs=vmem,
        scratch_shapes=[pltpu.VMEM((slots * rows, depth), jnp.bfloat16)],
        cost_estimate=pl.CostEstimate(
            flops=2 * slots * rows * depth * width,
            bytes_accessed=2 * (2 * tiles * rows * depth + depth * width + slots * rows * width),
            transcendentals=0,
        ),
        name="contract",
    )(panel, listed, own, sibling, green)


def virtual_kernel(message, own, sibling, before, total):
    tiles = own.shape[0]
    rows = total.shape[0]
    slots = (message.shape[0] - LABEL_ROWS) // rows
    labels = message[slots * rows :, :].astype(jnp.float32)
    line = lax.broadcasted_iota(jnp.int32, labels.shape, 0)
    result = before[...]
    for slot in range(slots):
        label = jnp.max(jnp.where(line == slot, labels, 0.0)).astype(jnp.int32)
        half, start = (own, 0) if slot < CAP else (sibling, tiles)
        place = jnp.clip(label - start, 0, tiles - 1)
        result = result + jnp.dot(
            message[slot * rows : (slot + 1) * rows, :], half[place], preferred_element_type=jnp.float32
        )
    total[...] = result


def virtual_product(message, own, sibling, before):
    vmem = pl.BlockSpec(memory_space=pltpu.VMEM)
    rows, columns = before.shape
    return pl.pallas_call(
        virtual_kernel,
        out_shape=jax.ShapeDtypeStruct(before.shape, jnp.float32),
        in_specs=[vmem] * 4,
        out_specs=vmem,
        cost_estimate=pl.CostEstimate(
            flops=2 * message.shape[0] * message.shape[1] * columns,
            bytes_accessed=2 * (message.size + own.size + sibling.size) + 8 * before.size,
            transcendentals=0,
        ),
        name="virtual_product",
    )(message, own, sibling, before)


def shards(integrals, green_occ, tile_panels, virtual_blocks):
    grid_count, rep_count = lax.axis_size("grid"), lax.axis_size("rep")
    pairs = rep_count // 2
    share = grid_count // rep_count
    tile_count = tile_panels.shape[0]
    rows = integrals.shape[0] // tile_count
    place, rep = lax.axis_index("grid"), lax.axis_index("rep")

    def offset(at, turn, k):
        return (at % 2) * (grid_count // 2) + ((at // 2) ^ turn) * share + k

    def send(array, target):
        order = []
        for g in range(grid_count):
            for r in range(rep_count):
                to_g, to_r = target(g, r)
                order.append((g * rep_count + r, to_g * rep_count + to_r))
        return lax.ppermute(array, AXES, order)

    def to_sibling(array):
        return send(array, lambda g, r: (g, r ^ 1))

    panels = {}
    for k in range(share):
        panels[0, k] = send(green_occ, lambda g, r, k=k: (g ^ offset(r, 0, k), r))
    own_tiles = integrals.reshape(tile_count, rows, -1)
    sibling_tiles = to_sibling(own_tiles)
    listed = jnp.stack([tile_panels, to_sibling(tile_panels)])
    own_virtual = virtual_blocks[0]
    sibling_virtual = to_sibling(own_virtual)
    for turn in range(1, pairs):
        for k in range(share):
            panels[turn, k] = send(panels[0, k], lambda g, r, t=turn: (g, r ^ (2 * t)))

    messages = []
    for turn in range(pairs):
        for k in range(share):
            panel = (place ^ offset(rep, turn, k)).astype(jnp.int32).reshape(1)
            message = contract(panel, listed, own_tiles, sibling_tiles, panels[turn, k])
            messages.append(send(message, lambda g, r, t=turn, k=k: (g ^ offset(r, t, k), r)))

    total = jnp.zeros((rows, virtual_blocks.shape[-1]), jnp.float32)
    for message in messages:
        total = virtual_product(message, own_virtual, sibling_virtual, total)

    step = rep_count // 2
    while step:
        half = total.shape[0] // 2
        low, high = total[:half], total[half:]
        upper = (rep // step) % 2 == 1
        kept, given = jnp.where(upper, high, low), jnp.where(upper, low, high)
        total = kept + send(given, lambda g, r, s=step: (g, r ^ s))
        step //= 2
    return total[None]


def solution(mesh):
    in_specs = (
        P(("grid", "rep"), None),
        P(None, "grid"),
        P(("grid", "rep"), None),
        P("grid", "rep", None, None),
    )
    out_specs = P("grid", "rep", None)
    return jax.shard_map(shards, mesh=mesh, in_specs=in_specs, out_specs=out_specs, check_vma=False)
```

```python
import functools

import jax
import jax.numpy as jnp
from jax import lax
from jax.experimental import pallas as pl
from jax.experimental.pallas import tpu as pltpu
from jax.sharding import PartitionSpec as P

AXES = ("grid", "rep")
CAP = 2
KERNEL_VMEM = 16 << 20
LABEL_ROWS = 16


def contract_kernel(panel, listed, own, sibling, green, message, chosen):
    tiles, rows, _ = own.shape
    hits = []
    for block, source in enumerate((own, sibling)):
        picks, count = [jnp.int32(0)] * CAP, jnp.int32(0)
        for tile in range(tiles):
            hit = functools.reduce(
                jnp.logical_or, [listed[block, tile, s] == panel[0] for s in range(listed.shape[2])]
            )
            picks = [jnp.where(hit & (count == n), tile, pick) for n, pick in enumerate(picks)]
            count = count + hit.astype(jnp.int32)
        for n, pick in enumerate(picks):
            slot = block * CAP + n
            chosen[slot * rows : (slot + 1) * rows, :] = source[pick]
            hits.append((n < count, block * tiles + pick))
    product = jnp.dot(chosen[...], green[...], preferred_element_type=jnp.float32)
    width = message.shape[1]
    line = lax.broadcasted_iota(jnp.int32, (LABEL_ROWS, width), 0)
    labels = jnp.zeros((LABEL_ROWS, width), jnp.float32)
    for slot, (used, label) in enumerate(hits):
        part = product[slot * rows : (slot + 1) * rows]
        part = jnp.where(used, part, jnp.zeros_like(part))
        message[slot * rows : (slot + 1) * rows, :] = part.astype(message.dtype)
        labels = jnp.where((line == slot) & used, label.astype(jnp.float32), labels)
    message[len(hits) * rows :, :] = labels.astype(message.dtype)


def contract(panel, listed, own, sibling, green):
    tiles, rows, depth = own.shape
    slots, width = 2 * CAP, green.shape[1]
    smem, vmem = pl.BlockSpec(memory_space=pltpu.SMEM), pl.BlockSpec(memory_space=pltpu.VMEM)
    return pl.pallas_call(
        contract_kernel,
        out_shape=jax.ShapeDtypeStruct((slots * rows + LABEL_ROWS, width), jnp.bfloat16),
        in_specs=[smem, smem, vmem, vmem, vmem],
        out_specs=vmem,
        scratch_shapes=[pltpu.VMEM((slots * rows, depth), jnp.bfloat16)],
        cost_estimate=pl.CostEstimate(
            flops=2 * slots * rows * depth * width,
            bytes_accessed=2 * (2 * tiles * rows * depth + depth * width + slots * rows * width),
            transcendentals=0,
        ),
        compiler_params=pltpu.CompilerParams(vmem_limit_bytes=KERNEL_VMEM),
        name="contract",
    )(panel, listed, own, sibling, green)


def virtual_kernel(message, own, sibling, before, total):
    tiles = own.shape[0]
    rows = total.shape[0]
    slots = (message.shape[0] - LABEL_ROWS) // rows
    labels = message[slots * rows :, :].astype(jnp.float32)
    line = lax.broadcasted_iota(jnp.int32, labels.shape, 0)
    result = before[...]
    for slot in range(slots):
        label = jnp.max(jnp.where(line == slot, labels, 0.0)).astype(jnp.int32)
        half, start = (own, 0) if slot < CAP else (sibling, tiles)
        place = jnp.clip(label - start, 0, tiles - 1)
        result = result + jnp.dot(
            message[slot * rows : (slot + 1) * rows, :], half[place], preferred_element_type=jnp.float32
        )
    total[...] = result


def virtual_product(message, own, sibling, before):
    vmem = pl.BlockSpec(memory_space=pltpu.VMEM)
    rows, columns = before.shape
    return pl.pallas_call(
        virtual_kernel,
        out_shape=jax.ShapeDtypeStruct(before.shape, jnp.float32),
        in_specs=[vmem] * 4,
        out_specs=vmem,
        cost_estimate=pl.CostEstimate(
            flops=2 * message.shape[0] * message.shape[1] * columns,
            bytes_accessed=2 * (message.size + own.size + sibling.size) + 8 * before.size,
            transcendentals=0,
        ),
        compiler_params=pltpu.CompilerParams(vmem_limit_bytes=KERNEL_VMEM),
        name="virtual_product",
    )(message, own, sibling, before)


def shards(integrals, green_occ, tile_panels, virtual_blocks):
    grid_count, rep_count = lax.axis_size("grid"), lax.axis_size("rep")
    pairs = rep_count // 2
    share = grid_count // rep_count
    tile_count = tile_panels.shape[0]
    rows = integrals.shape[0] // tile_count
    place, rep = lax.axis_index("grid"), lax.axis_index("rep")

    def offset(at, turn, k):
        return (at % 2) * (grid_count // 2) + ((at // 2) ^ turn) * share + k

    def send(array, target):
        order = []
        for g in range(grid_count):
            for r in range(rep_count):
                to_g, to_r = target(g, r)
                order.append((g * rep_count + r, to_g * rep_count + to_r))
        return lax.ppermute(array, AXES, order)

    def to_sibling(array):
        return send(array, lambda g, r: (g, r ^ 1))

    panels = {}
    for k in range(share):
        panels[0, k] = send(green_occ, lambda g, r, k=k: (g ^ offset(r, 0, k), r))
    own_tiles = integrals.reshape(tile_count, rows, -1)
    sibling_tiles = to_sibling(own_tiles)
    listed = jnp.stack([tile_panels, to_sibling(tile_panels)])
    own_virtual = virtual_blocks[0]
    sibling_virtual = to_sibling(own_virtual)
    for turn in range(1, pairs):
        for k in range(share):
            panels[turn, k] = send(panels[0, k], lambda g, r, t=turn: (g, r ^ (2 * t)))

    messages = []
    for turn in range(pairs):
        for k in range(share):
            panel = (place ^ offset(rep, turn, k)).astype(jnp.int32).reshape(1)
            message = contract(panel, listed, own_tiles, sibling_tiles, panels[turn, k])
            messages.append(send(message, lambda g, r, t=turn, k=k: (g ^ offset(r, t, k), r)))

    total = jnp.zeros((rows, virtual_blocks.shape[-1]), jnp.float32)
    for message in messages:
        total = virtual_product(message, own_virtual, sibling_virtual, total)

    step = rep_count // 2
    while step:
        half = total.shape[0] // 2
        low, high = total[:half], total[half:]
        upper = (rep // step) % 2 == 1
        kept, given = jnp.where(upper, high, low), jnp.where(upper, low, high)
        total = kept + send(given, lambda g, r, s=step: (g, r ^ s))
        step //= 2
    return total[None]


def solution(mesh):
    in_specs = (
        P(("grid", "rep"), None),
        P(None, "grid"),
        P(("grid", "rep"), None),
        P("grid", "rep", None, None),
    )
    out_specs = P("grid", "rep", None)
    return jax.shard_map(shards, mesh=mesh, in_specs=in_specs, out_specs=out_specs, check_vma=False)
```

```python
import jax
import jax.numpy as jnp
from jax import lax
from jax.experimental import pallas as pl
from jax.experimental.pallas import tpu as pltpu
from jax.sharding import PartitionSpec as P

AXES = ("grid", "rep")
KERNEL_VMEM = 16 << 20
SQUARE = 4
CHUNK = 2
VMEM = pl.BlockSpec(memory_space=pltpu.VMEM)
SMEM = pl.BlockSpec(memory_space=pltpu.SMEM)


def sources_of(own, first, second, corner_head, corner_tail, rows):
    labels = own.shape[0] - CHUNK * rows
    places = []
    for array in (own, first, second):
        tiles = [array[labels + n * rows : labels + (n + 1) * rows, :] for n in range(CHUNK)]
        places.append((array[:labels, :], tiles))
    places.append((corner_head[:labels, :], [corner_head[labels:, :], corner_tail[...]]))
    return places


def masked_products(panel, places, green, picks):
    width = green.shape[1]
    wanted = panel.astype(jnp.float32)
    products = []
    for labels, tiles in places:
        named = (labels[:, :width].astype(jnp.float32) == wanted).astype(jnp.float32)
        line = []
        for n, tile in enumerate(tiles):
            hit = jnp.max(named[n * picks : (n + 1) * picks], axis=0, keepdims=True)
            product = jnp.dot(tile, green, preferred_element_type=jnp.float32)
            line.append((product * hit).astype(jnp.bfloat16))
        products.append(line)
    return products


def far_kernel(picks, panel, part, own, first, second, corner_head, corner_tail, kept, swapped, message, green):
    rows, half = message.shape[0] // CHUNK, kept.shape[0]
    green[pl.ds(part[0] * half, half), :] = kept[...]
    green[pl.ds((1 - part[0]) * half, half), :] = swapped[...]
    places = sources_of(own, first, second, corner_head, corner_tail, rows)
    products = masked_products(panel[0], places, green[...], picks)
    for n in range(CHUNK):
        total = sum(line[n].astype(jnp.float32) for line in products)
        message[n * rows : (n + 1) * rows, :] = total.astype(message.dtype)


def near_kernel(picks, panel, own, first, second, corner_head, corner_tail, green, virtual, before, total):
    rows = before.shape[0]
    places = sources_of(own, first, second, corner_head, corner_tail, rows)
    products = masked_products(panel[0], places, green[...], picks)
    result = before[...]
    for n in range(CHUNK):
        for line in products:
            result = result + jnp.dot(line[n], virtual[n], preferred_element_type=jnp.float32)
    total[...] = result


def virtual_kernel(message, virtual, before, total):
    rows = before.shape[0]
    result = before[...]
    for n in range(CHUNK):
        result = result + jnp.dot(
            message[n * rows : (n + 1) * rows, :], virtual[n], preferred_element_type=jnp.float32
        )
    total[...] = result


def call(kernel, name, out, specs, flops, scratch=()):
    def run(*operands):
        moved = sum(operand.size * operand.dtype.itemsize for operand in operands)
        return pl.pallas_call(
            kernel,
            out_shape=out,
            in_specs=specs,
            out_specs=VMEM,
            scratch_shapes=scratch,
            cost_estimate=pl.CostEstimate(flops=flops, bytes_accessed=moved, transcendentals=0),
            compiler_params=pltpu.CompilerParams(vmem_limit_bytes=KERNEL_VMEM),
            name=name,
        )(*operands)

    return run


def shards(integrals, green_occ, tile_panels, virtual_blocks):
    grid_count, rep_count = lax.axis_size("grid"), lax.axis_size("rep")
    tile_count, picks = tile_panels.shape
    rows, depth = integrals.shape[0] // tile_count, integrals.shape[1]
    width, columns = virtual_blocks.shape[-2:]
    place, rep = lax.axis_index("grid"), lax.axis_index("rep")

    def send(array, grid_bits, rep_bits=0):
        order = []
        for g in range(grid_count):
            for r in range(rep_count):
                order.append((g * rep_count + r, (g ^ grid_bits) * rep_count + (r ^ rep_bits)))
        return lax.ppermute(array, AXES, order)

    def scalar(value):
        return value.astype(jnp.int32).reshape(1)

    label_rows = -(-CHUNK * picks // 16) * 16
    chunks = range(tile_count // CHUNK)
    own, first, second = [], [], []
    part = rep % 2
    half = green_occ.shape[0] // 2
    mine = lax.dynamic_slice_in_dim(green_occ, part * half, half, 0)
    kept = {}
    for n in chunks:
        named = tile_panels[n * CHUNK : (n + 1) * CHUNK].reshape(CHUNK * picks, 1).astype(jnp.bfloat16)
        named = jnp.pad(named, ((0, label_rows - CHUNK * picks), (0, 0)), constant_values=-1)
        tiles = integrals[n * CHUNK * rows : (n + 1) * CHUNK * rows]
        own.append(jnp.concatenate([jnp.broadcast_to(named, (label_rows, depth)), tiles], axis=0))
        first.append(send(own[n], 1))
        second.append(send(own[n], 2))
        if n == 0:
            for far in range(SQUARE, grid_count, SQUARE):
                kept[far] = send(mine, far)
    swapped = {far: send(array, 0, 1) for far, array in kept.items()}

    cut = label_rows + rows
    heads = [send(first[n][:cut], 2) for n in chunks]
    tails = [send(second[n][cut:], 1) for n in chunks]
    square = [(own[n], first[n], second[n], heads[n], tails[n]) for n in chunks]

    tile_flops = 2 * rows * depth * width
    messages = []
    for n in chunks:
        for far in kept:
            contract = call(
                lambda *refs: far_kernel(picks, *refs),
                "far_panel",
                jax.ShapeDtypeStruct((CHUNK * rows, width), jnp.bfloat16),
                [SMEM, SMEM] + [VMEM] * 7,
                SQUARE * CHUNK * tile_flops,
                [pltpu.VMEM((depth, width), jnp.bfloat16)],
            )
            message = contract(scalar(place ^ far), scalar(part), *square[n], kept[far], swapped[far])
            messages.append((n, send(message, far)))

    sums = jax.ShapeDtypeStruct((rows, columns), jnp.float32)
    total = jnp.zeros(sums.shape, sums.dtype)
    blocks = [virtual_blocks[0, n * CHUNK : (n + 1) * CHUNK] for n in chunks]
    for n in chunks:
        near = call(
            lambda *refs: near_kernel(picks, *refs),
            "own_panel",
            sums,
            [SMEM] + [VMEM] * 8,
            SQUARE * CHUNK * (tile_flops + 2 * rows * width * columns),
        )
        total = near(scalar(place), *square[n], green_occ, blocks[n], total)
    for n, message in messages:
        product = call(virtual_kernel, "virtual_product", sums, [VMEM] * 3, 2 * CHUNK * rows * width * columns)
        total = product(message, blocks[n], total)

    step = rep_count // 2
    while step:
        middle = total.shape[0] // 2
        low, high = total[:middle], total[middle:]
        upper = (rep // step) % 2 == 1
        stays, leaves = jnp.where(upper, high, low), jnp.where(upper, low, high)
        total = stays + send(leaves, 0, step)
        step //= 2
    return total[None]


def solution(mesh):
    in_specs = (
        P(("grid", "rep"), None),
        P(None, "grid"),
        P(("grid", "rep"), None),
        P("grid", "rep", None, None),
    )
    out_specs = P("grid", "rep", None)
    return jax.shard_map(shards, mesh=mesh, in_specs=in_specs, out_specs=out_specs, check_vma=False)
```

```python
import jax
import jax.numpy as jnp
from jax import lax
from jax.experimental import pallas as pl
from jax.experimental.pallas import tpu as pltpu
from jax.sharding import PartitionSpec as P

AXES = ("grid", "rep")
KERNEL_VMEM = 16 << 20
PACK_VMEM = 56 << 20
SQUARE = 4
CHUNK = 2
VMEM = pl.BlockSpec(memory_space=pltpu.VMEM)
ANY = pl.BlockSpec(memory_space=pl.ANY)
HBM = pl.BlockSpec(memory_space=pltpu.HBM)


def position():
    rep = lax.axis_index("rep")
    return lax.axis_index("grid"), rep // 2, rep % 2


def pack_kernel(picks, listed, integrals, green, half_green, *rest):
    *messages, names, done = rest
    half = half_green.shape[0]
    tile_rows = integrals.shape[0] // len(messages)
    label_rows = messages[0].shape[0] - tile_rows
    start = pl.multiple_of(position()[2] * half, half)
    copies = [
        pltpu.make_async_copy(listed, names, done.at[0]),
        pltpu.make_async_copy(green.at[pl.ds(start, half), :], half_green, done.at[1]),
    ]
    for m, message in enumerate(messages):
        copies.append(
            pltpu.make_async_copy(
                integrals.at[m * tile_rows : (m + 1) * tile_rows, :],
                message.at[label_rows:, :],
                done.at[m + 2],
            )
        )
    for copy in copies:
        copy.start()
    copies[0].wait()
    line = lax.broadcasted_iota(jnp.int32, (label_rows, messages[0].shape[1]), 0)
    for m, message in enumerate(messages):
        value = jnp.full(line.shape, -1, jnp.int32)
        for n in range(CHUNK):
            for s in range(picks):
                tile = m * CHUNK + n
                value = jnp.where(line == n * picks + s, names[s : s + 1, tile : tile + 1], value)
        message[:label_rows, :] = value.astype(jnp.float32).astype(message.dtype)
    for copy in copies[1:]:
        copy.wait()


def join_kernel(own, *rest):
    *halves, panels = rest
    half = halves[0].shape[0]
    core = position()[2]
    panels[0] = own[...]
    for n in range(len(halves) // 2):
        for h, array in enumerate(halves[2 * n : 2 * n + 2]):
            start = pl.multiple_of((core ^ h) * half, half)
            panels[1 + n, pl.ds(start, half), :] = array[...]


def sums_kernel(picks, fars, own, first, second, corner, panels, after, *rest):
    *messages, total = rest
    pairs = len(messages) // len(fars)
    share = messages[0].shape[0] // CHUNK
    rows, width = share * pairs, panels.shape[2]
    labels = own.shape[0] - CHUNK * rows
    place, x, _ = position()
    sources = [own, first, second, corner]
    names = [source[:labels, :width].astype(jnp.float32) for source in sources]
    for p, far in enumerate(fars):
        wanted = (place ^ far).astype(jnp.float32)
        green = panels[p]
        for n in range(CHUNK):
            sums = jnp.zeros((rows, width), jnp.float32)
            for source, name in zip(sources, names):
                named = (name[n * picks : (n + 1) * picks] == wanted).astype(jnp.float32)
                hit = jnp.max(named, axis=0, keepdims=True)
                tile = source[labels + n * rows : labels + (n + 1) * rows, :]
                product = jnp.dot(tile, green, preferred_element_type=jnp.float32) * hit
                sums = sums + product.astype(jnp.bfloat16).astype(jnp.float32)
            total[n] = sums
        for t in range(pairs):
            start = pl.multiple_of((x ^ t) * share, share)
            for n in range(CHUNK):
                block = total[n, pl.ds(start, share), :]
                message = messages[p * pairs + t]
                message[n * share : (n + 1) * share, :] = block.astype(message.dtype)


def virtual_sum(rows, operands):
    result = None
    for message, virtual in zip(operands[::2], operands[1::2]):
        for n in range(CHUNK):
            tile = message[n * rows : (n + 1) * rows, :]
            product = jnp.dot(tile, virtual[n], preferred_element_type=jnp.float32)
            result = product if result is None else result + product
    return result


def first_kernel(*refs):
    *operands, total = refs
    total[...] = virtual_sum(total.shape[0], operands)


def last_kernel(before, *refs):
    *operands, stays, leaves, total = refs
    middle = stays.shape[0]
    total[...] = before[...] + virtual_sum(total.shape[0], operands)
    core = position()[2]
    stays[...] = total[pl.ds(pl.multiple_of(core * middle, middle), middle), :]
    leaves[...] = total[pl.ds(pl.multiple_of((1 - core) * middle, middle), middle), :]


def call(kernel, name, out, specs, flops, scratch=(), vmem=KERNEL_VMEM):
    def run(*operands):
        return pl.pallas_call(
            kernel,
            out_shape=out,
            in_specs=specs,
            out_specs=jax.tree.map(lambda _: VMEM, out),
            scratch_shapes=scratch,
            cost_estimate=pl.CostEstimate(flops=flops, bytes_accessed=0, transcendentals=0),
            compiler_params=pltpu.CompilerParams(vmem_limit_bytes=vmem),
            name=name,
        )(*operands)

    return run


def shards(integrals, green_occ, tile_panels, virtual_blocks):
    grid_count, rep_count = lax.axis_size("grid"), lax.axis_size("rep")
    pairs = rep_count // 2
    tile_count, picks = tile_panels.shape
    rows, depth = integrals.shape[0] // tile_count, integrals.shape[1]
    width, columns = virtual_blocks.shape[-2:]
    share = rows // pairs

    def send(array, grid_bits, rep_bits=0):
        order = []
        for g in range(grid_count):
            for r in range(rep_count):
                order.append((g * rep_count + r, (g ^ grid_bits) * rep_count + (r ^ rep_bits)))
        return lax.ppermute(array, AXES, order)

    def like(shape, dtype):
        return jax.ShapeDtypeStruct(shape, dtype)

    label_rows = -(-CHUNK * picks // 16) * 16
    chunks = range(tile_count // CHUNK)
    half = green_occ.shape[0] // 2
    outs = [like((half, green_occ.shape[1]), green_occ.dtype)]
    outs += [like((label_rows + CHUNK * rows, depth), integrals.dtype) for _ in chunks]
    scratch = [
        pltpu.VMEM((picks, tile_count), jnp.int32),
        pltpu.SemaphoreType.DMA((2 + len(chunks),)),
    ]
    pack = call(lambda *refs: pack_kernel(picks, *refs), "pack", outs, [HBM] * 3, 0, scratch, PACK_VMEM)
    mine, *own = pack(tile_panels.T, integrals, green_occ)

    near = [n % 2 == 1 for n in chunks]
    first, second, corner = {}, {}, {}
    for wanted in (True, False):
        for n in chunks:
            if near[n] == wanted:
                second[n] = send(own[n], 2)
            else:
                first[n] = send(own[n], 1)
        if wanted:
            fars = list(range(SQUARE, grid_count, SQUARE))
            kept = [send(mine, far) for far in fars]
    for n in chunks:
        corner[n] = send(second[n], 1) if near[n] else send(first[n], 2)
    halves = [array for one in kept for array in (one, send(one, 0, 1))]
    fars = [0] + fars
    join = call(
        join_kernel,
        "join",
        like((len(fars),) + green_occ.shape, green_occ.dtype),
        [VMEM] * (1 + len(halves)),
        5 * 10**9,
    )
    panels = join(green_occ, *halves)

    virtual = [virtual_blocks[0]]
    virtual += [send(virtual[0], 0, 2 * t) for t in range(1, pairs)]

    after, operands = mine, {}
    ordered = sorted(chunks, key=lambda n: not near[n])
    for n in ordered:
        outs = [like((CHUNK * share, width), jnp.bfloat16)] * (len(fars) * pairs)
        sums = call(
            lambda *refs: sums_kernel(picks, fars, *refs),
            "sums",
            outs,
            [VMEM] * 5 + [ANY],
            2 * 10**9,
            [pltpu.VMEM((CHUNK, rows, width), jnp.float32)],
        )
        parts = sums(own[n], first[n], second[n], corner[n], panels, after)
        after = parts[0]
        operands[n] = []
        for p, far in enumerate(fars):
            for t in range(pairs):
                part = parts[p * pairs + t]
                message = send(part, far, 2 * t) if far or t else part
                operands[n] += [message, virtual[t][n * CHUNK : (n + 1) * CHUNK]]

    *early, late = ordered
    operands_of = [array for n in early for array in operands[n]]
    part = call(
        first_kernel, "virtual_first", like((share, columns), jnp.float32), [VMEM] * len(operands_of), 10**10
    )(*operands_of)
    last = call(
        last_kernel,
        "virtual_last",
        [like((share // 2, columns), jnp.float32)] * 2,
        [VMEM] * (1 + len(operands[late])),
        0,
        [pltpu.VMEM((share, columns), jnp.float32)],
    )
    stays, leaves = last(part, *operands[late])
    return (stays + send(leaves, 0, 1))[None]


def solution(mesh):
    in_specs = (
        P(("grid", "rep"), None),
        P(None, "grid"),
        P(("grid", "rep"), None),
        P("grid", "rep", None, None),
    )
    out_specs = P("grid", "rep", None)
    return jax.shard_map(shards, mesh=mesh, in_specs=in_specs, out_specs=out_specs, check_vma=False)
```

```python
import jax
import jax.numpy as jnp
from jax import lax
from jax.experimental import pallas as pl
from jax.experimental.pallas import tpu as pltpu
from jax.sharding import PartitionSpec as P

AXES = ("grid", "rep")
KERNEL_VMEM = 16 << 20
PACK_VMEM = 56 << 20
SQUARE = 4
CHUNK = 2
VMEM = pl.BlockSpec(memory_space=pltpu.VMEM)
ANY = pl.BlockSpec(memory_space=pl.ANY)
HBM = pl.BlockSpec(memory_space=pltpu.HBM)


def position():
    rep = lax.axis_index("rep")
    return lax.axis_index("grid"), rep // 2, rep % 2


def pack_kernel(picks, listed, integrals, green, half_green, *rest):
    whole, *messages, names, done = rest
    half = half_green.shape[0]
    size = messages[0].shape[0]
    tile_rows = integrals.shape[0] // len(messages)
    label_rows = size - tile_rows
    start = pl.multiple_of(position()[2] * half, half)
    copies = [
        pltpu.make_async_copy(listed, names, done.at[0]),
        pltpu.make_async_copy(green.at[pl.ds(start, half), :], half_green, done.at[1]),
    ]
    for m, message in enumerate(messages):
        tiles = integrals.at[m * tile_rows : (m + 1) * tile_rows, :]
        copies.append(pltpu.make_async_copy(tiles, message.at[label_rows:, :], done.at[2 * m + 2]))
        place = whole.at[m * size + label_rows : (m + 1) * size, :]
        copies.append(pltpu.make_async_copy(tiles, place, done.at[2 * m + 3]))
    for copy in copies:
        copy.start()
    copies[0].wait()
    line = lax.broadcasted_iota(jnp.int32, (label_rows, messages[0].shape[1]), 0)
    for m, message in enumerate(messages):
        value = jnp.full(line.shape, -1, jnp.int32)
        for n in range(CHUNK):
            for s in range(picks):
                tile = m * CHUNK + n
                value = jnp.where(line == n * picks + s, names[s : s + 1, tile : tile + 1], value)
        labels = value.astype(jnp.float32).astype(message.dtype)
        message[:label_rows, :] = labels
        whole[m * size : m * size + label_rows, :] = labels
    for copy in copies[1:]:
        copy.wait()


def join_kernel(own, *rest):
    *halves, panels = rest
    half = halves[0].shape[0]
    core = position()[2]
    panels[len(halves) // 2] = own[...]
    for n in range(len(halves) // 2):
        for h, array in enumerate(halves[2 * n : 2 * n + 2]):
            start = pl.multiple_of((core ^ h) * half, half)
            panels[n, pl.ds(start, half), :] = array[...]


def sums_kernel(picks, fars, chunk, own, first, second, corner, panels, after, *rest):
    *messages, total = rest
    pairs = len(messages) // len(fars)
    share = messages[0].shape[0] // CHUNK
    rows, width = share * pairs, panels.shape[2]
    labels = own.shape[0] - CHUNK * rows
    place, x, _ = position()
    sources = [(own, 0), (first, chunk * own.shape[0]), (second, 0), (corner, 0)]
    names = [source[at : at + labels, :width].astype(jnp.float32) for source, at in sources]
    for p, far in enumerate(fars):
        wanted = (place ^ far).astype(jnp.float32)
        green = panels[p]
        for n in range(CHUNK):
            sums = jnp.zeros((rows, width), jnp.float32)
            for (source, at), name in zip(sources, names):
                named = (name[n * picks : (n + 1) * picks] == wanted).astype(jnp.float32)
                hit = jnp.max(named, axis=0, keepdims=True)
                start = at + labels + n * rows
                tile = source[start : start + rows, :]
                product = jnp.dot(tile, green, preferred_element_type=jnp.float32) * hit
                sums = sums + product.astype(jnp.bfloat16).astype(jnp.float32)
            total[n] = sums
        for t in range(pairs):
            start = pl.multiple_of((x ^ t) * share, share)
            for n in range(CHUNK):
                block = total[n, pl.ds(start, share), :]
                message = messages[p * pairs + t]
                message[n * share : (n + 1) * share, :] = block.astype(message.dtype)


def virtual_sum(rows, operands):
    result = None
    for message, virtual in zip(operands[::2], operands[1::2]):
        for n in range(CHUNK):
            tile = message[n * rows : (n + 1) * rows, :]
            product = jnp.dot(tile, virtual[n], preferred_element_type=jnp.float32)
            result = product if result is None else result + product
    return result


def first_kernel(*refs):
    *operands, total = refs
    total[...] = virtual_sum(total.shape[0], operands)


def last_kernel(before, *refs):
    *operands, stays, leaves, total = refs
    middle = stays.shape[0]
    total[...] = before[...] + virtual_sum(total.shape[0], operands)
    core = position()[2]
    stays[...] = total[pl.ds(pl.multiple_of(core * middle, middle), middle), :]
    leaves[...] = total[pl.ds(pl.multiple_of((1 - core) * middle, middle), middle), :]


def call(kernel, name, out, specs, flops, scratch=(), vmem=KERNEL_VMEM):
    def run(*operands):
        return pl.pallas_call(
            kernel,
            out_shape=out,
            in_specs=specs,
            out_specs=jax.tree.map(lambda _: VMEM, out),
            scratch_shapes=scratch,
            cost_estimate=pl.CostEstimate(flops=flops, bytes_accessed=0, transcendentals=0),
            compiler_params=pltpu.CompilerParams(vmem_limit_bytes=vmem),
            name=name,
        )(*operands)

    return run


def shards(integrals, green_occ, tile_panels, virtual_blocks):
    grid_count, rep_count = lax.axis_size("grid"), lax.axis_size("rep")
    pairs = rep_count // 2
    tile_count, picks = tile_panels.shape
    rows, depth = integrals.shape[0] // tile_count, integrals.shape[1]
    width, columns = virtual_blocks.shape[-2:]
    share = rows // pairs

    def send(array, grid_bits, rep_bits=0):
        order = []
        for g in range(grid_count):
            for r in range(rep_count):
                order.append((g * rep_count + r, (g ^ grid_bits) * rep_count + (r ^ rep_bits)))
        return lax.ppermute(array, AXES, order)

    def like(shape, dtype):
        return jax.ShapeDtypeStruct(shape, dtype)

    label_rows = -(-CHUNK * picks // 16) * 16
    chunks = range(tile_count // CHUNK)
    half = green_occ.shape[0] // 2
    outs = [like((half, green_occ.shape[1]), green_occ.dtype)]
    size = label_rows + CHUNK * rows
    outs.append(like((len(chunks) * size, depth), integrals.dtype))
    outs += [like((size, depth), integrals.dtype) for _ in chunks]
    scratch = [
        pltpu.VMEM((picks, tile_count), jnp.int32),
        pltpu.SemaphoreType.DMA((2 + 2 * len(chunks),)),
    ]
    pack = call(lambda *refs: pack_kernel(picks, *refs), "pack", outs, [HBM] * 3, 0, scratch, PACK_VMEM)
    mine, whole, *own = pack(tile_panels.T, integrals, green_occ)

    near = [n % 2 == 1 for n in chunks]
    first = send(whole, 1)
    second = {n: send(own[n], 2) for wanted in (True, False) for n in chunks if near[n] == wanted}
    fars = list(range(SQUARE, grid_count, SQUARE))
    kept = [send(mine, far) for far in fars]
    corner = {}
    for n in chunks:
        corner[n] = send(second[n], 1) if near[n] else send(first[n * size : (n + 1) * size], 2)
    halves = [array for one in kept for array in (one, send(one, 0, 1))]
    fars = fars + [0]
    join = call(
        join_kernel,
        "join",
        like((len(fars),) + green_occ.shape, green_occ.dtype),
        [VMEM] * (1 + len(halves)),
        0,
    )
    panels = join(green_occ, *halves)

    virtual = [virtual_blocks[0]]
    virtual += [send(virtual[0], 0, 2 * t) for t in range(1, pairs)]

    after, operands = mine, {}
    ordered = sorted(chunks, key=lambda n: not near[n])
    for n in ordered:
        outs = [like((CHUNK * share, width), jnp.bfloat16)] * (len(fars) * pairs)
        sums = call(
            lambda *refs, n=n: sums_kernel(picks, fars, n, *refs),
            "sums",
            outs,
            [VMEM] * 5 + [ANY],
            0,
            [pltpu.VMEM((CHUNK, rows, width), jnp.float32)],
        )
        parts = sums(own[n], first, second[n], corner[n], panels, after)
        after = parts[0]
        operands[n] = []
        for p, far in enumerate(fars):
            for t in range(pairs):
                part = parts[p * pairs + t]
                message = send(part, far, 2 * t) if far or t else part
                operands[n] += [message, virtual[t][n * CHUNK : (n + 1) * CHUNK]]

    *early, late = ordered
    operands_of = [array for n in early for array in operands[n]]
    part = call(
        first_kernel, "virtual_first", like((share, columns), jnp.float32), [VMEM] * len(operands_of), 10**9
    )(*operands_of)
    last = call(
        last_kernel,
        "virtual_last",
        [like((share // 2, columns), jnp.float32)] * 2,
        [VMEM] * (1 + len(operands[late])),
        0,
        [pltpu.VMEM((share, columns), jnp.float32)],
    )
    stays, leaves = last(part, *operands[late])
    return (stays + send(leaves, 0, 1))[None]


def solution(mesh):
    in_specs = (
        P(("grid", "rep"), None),
        P(None, "grid"),
        P(("grid", "rep"), None),
        P("grid", "rep", None, None),
    )
    out_specs = P("grid", "rep", None)
    return jax.shard_map(shards, mesh=mesh, in_specs=in_specs, out_specs=out_specs, check_vma=False)
```

```python
import jax
import jax.numpy as jnp
from jax import lax
from jax.experimental import pallas as pl
from jax.experimental.pallas import tpu as pltpu
from jax.sharding import PartitionSpec as P

AXES = ("grid", "rep")
KERNEL_VMEM = 16 << 20
SQUARE = 4
CHUNK = 2
VMEM = pl.BlockSpec(memory_space=pltpu.VMEM)
ANY = pl.BlockSpec(memory_space=pl.ANY)


def position():
    rep = lax.axis_index("rep")
    return lax.axis_index("grid"), rep // 2, rep % 2


def half_kernel(green, half_green):
    half = half_green.shape[0]
    half_green[...] = green[pl.ds(pl.multiple_of(position()[2] * half, half), half), :]


def join_kernel(own, *rest):
    *halves, panels = rest
    half = halves[0].shape[0]
    core = position()[2]
    panels[len(halves) // 2] = own[...]
    for n in range(len(halves) // 2):
        for h, array in enumerate(halves[2 * n : 2 * n + 2]):
            start = pl.multiple_of((core ^ h) * half, half)
            panels[n, pl.ds(start, half), :] = array[...]


def add_products(picks, panel, green, sources, rows, sums):
    wanted, width = panel.astype(jnp.float32), green.shape[1]
    result = list(sums)
    for source, start, size in sources:
        labels = size - CHUNK * rows
        names = source[start : start + labels, :width].astype(jnp.float32)
        for n in range(CHUNK):
            named = (names[n * picks : (n + 1) * picks] == wanted).astype(jnp.float32)
            tile = source[start + labels + n * rows : start + labels + (n + 1) * rows, :]
            product = jnp.dot(tile, green, preferred_element_type=jnp.float32)
            product = (product * jnp.max(named, axis=0, keepdims=True)).astype(jnp.bfloat16)
            result[n] = result[n] + product.astype(jnp.float32)
    return result


def near_kernel(picks, chunk, own, first, second, green, total):
    rows, size = total.shape[1], own.shape[0]
    sources = [(own, 0, size), (first, chunk * size, size), (second, 0, size)]
    zeros = [jnp.zeros(total.shape[1:], jnp.float32)] * CHUNK
    for n, sums in enumerate(add_products(picks, position()[0], green[...], sources, rows, zeros)):
        total[n] = sums


def sums_kernel(picks, fars, chunk, own, first, second, corner, panels, near, after, *rest):
    *messages, total = rest
    pairs = len(messages) // len(fars)
    share = messages[0].shape[0] // CHUNK
    rows, width, size = share * pairs, panels.shape[2], own.shape[0]
    place, x, _ = position()
    every = [(own, 0, size), (first, chunk * size, size), (second, 0, size), (corner, 0, size)]
    for p, far in enumerate(fars):
        if far:
            sums, sources = [jnp.zeros((rows, width), jnp.float32)] * CHUNK, every
        else:
            sums, sources = [near[n] for n in range(CHUNK)], every[-1:]
        for n, one in enumerate(add_products(picks, place ^ far, panels[p], sources, rows, sums)):
            total[n] = one
        for t in range(pairs):
            start = pl.multiple_of((x ^ t) * share, share)
            for n in range(CHUNK):
                block = total[n, pl.ds(start, share), :]
                message = messages[p * pairs + t]
                message[n * share : (n + 1) * share, :] = block.astype(message.dtype)


def virtual_sum(rows, operands):
    result = None
    for message, virtual in zip(operands[::2], operands[1::2]):
        for n in range(CHUNK):
            tile = message[n * rows : (n + 1) * rows, :]
            product = jnp.dot(tile, virtual[n], preferred_element_type=jnp.float32)
            result = product if result is None else result + product
    return result


def first_kernel(*refs):
    *operands, total = refs
    total[...] = virtual_sum(total.shape[0], operands)


def last_kernel(before, *refs):
    *operands, stays, leaves, total = refs
    middle = stays.shape[0]
    total[...] = before[...] + virtual_sum(total.shape[0], operands)
    core = position()[2]
    stays[...] = total[pl.ds(pl.multiple_of(core * middle, middle), middle), :]
    leaves[...] = total[pl.ds(pl.multiple_of((1 - core) * middle, middle), middle), :]


def call(kernel, name, out, specs, flops, scratch=()):
    def run(*operands):
        return pl.pallas_call(
            kernel,
            out_shape=out,
            in_specs=specs,
            out_specs=jax.tree.map(lambda _: VMEM, out),
            scratch_shapes=scratch,
            cost_estimate=pl.CostEstimate(flops=flops, bytes_accessed=0, transcendentals=0),
            compiler_params=pltpu.CompilerParams(vmem_limit_bytes=KERNEL_VMEM),
            name=name,
        )(*operands)

    return run


def shards(integrals, green_occ, tile_panels, virtual_blocks):
    grid_count, rep_count = lax.axis_size("grid"), lax.axis_size("rep")
    pairs = rep_count // 2
    tile_count, picks = tile_panels.shape
    rows, depth = integrals.shape[0] // tile_count, integrals.shape[1]
    width, columns = virtual_blocks.shape[-2:]
    share = rows // pairs

    def send(array, grid_bits, rep_bits=0):
        order = []
        for g in range(grid_count):
            for r in range(rep_count):
                order.append((g * rep_count + r, (g ^ grid_bits) * rep_count + (r ^ rep_bits)))
        return lax.ppermute(array, AXES, order)

    def like(shape, dtype):
        return jax.ShapeDtypeStruct(shape, dtype)

    label_rows = -(-CHUNK * picks // 16) * 16
    chunks = range(tile_count // CHUNK)
    size = label_rows + CHUNK * rows
    half = like((green_occ.shape[0] // 2, green_occ.shape[1]), green_occ.dtype)
    mine = call(half_kernel, "half", half, [VMEM], 0)(green_occ)
    blocks = integrals.reshape(len(chunks), CHUNK * rows, depth)
    named = tile_panels.reshape(len(chunks), CHUNK * picks, 1).astype(jnp.bfloat16)
    named = jnp.pad(named, ((0, 0), (0, label_rows - CHUNK * picks), (0, 0)), constant_values=-1)
    named = jnp.broadcast_to(named, (len(chunks), label_rows, depth))
    whole = jnp.concatenate([named, blocks], axis=1)
    own = [whole[n] for n in chunks]
    whole = whole.reshape(len(chunks) * size, depth)

    near = [n % 2 == 1 for n in chunks]
    first = send(whole, 1)
    second = {n: send(own[n], 2) for wanted in (True, False) for n in chunks if near[n] == wanted}
    fars = list(range(SQUARE, grid_count, SQUARE))
    kept = [send(mine, far) for far in fars]
    corner = {}
    for n in chunks:
        corner[n] = send(second[n], 1) if near[n] else send(first[n * size : (n + 1) * size], 2)
    halves = [array for one in kept for array in (one, send(one, 0, 1))]
    fars = fars + [0]
    join = call(
        join_kernel,
        "join",
        like((len(fars),) + green_occ.shape, green_occ.dtype),
        [VMEM] * (1 + len(halves)),
        0,
    )
    panels = join(green_occ, *halves)

    virtual = [virtual_blocks[0]]
    virtual += [send(virtual[0], 0, 2 * t) for t in range(1, pairs)]

    after, operands = mine, {}
    ordered = sorted(chunks, key=lambda n: not near[n])
    for n in ordered:
        outs = [like((CHUNK * share, width), jnp.bfloat16)] * (len(fars) * pairs)
        sums = call(
            lambda *refs, n=n: sums_kernel(picks, fars, n, *refs),
            "sums",
            outs,
            [VMEM] * 6 + [ANY],
            0,
            [pltpu.VMEM((CHUNK, rows, width), jnp.float32)],
        )
        near_shape = like((CHUNK, rows, width), jnp.float32)
        part = call(
            lambda *refs, n=n: near_kernel(picks, n, *refs), "near", near_shape, [VMEM] * 4, 0
        )(own[n], first, second[n], green_occ)
        parts = sums(own[n], first, second[n], corner[n], panels, part, after)
        after = parts[0]
        operands[n] = []
        for p, far in enumerate(fars):
            for t in range(pairs):
                part = parts[p * pairs + t]
                message = send(part, far, 2 * t) if far or t else part
                operands[n] += [message, virtual[t][n * CHUNK : (n + 1) * CHUNK]]

    *early, late = ordered
    operands_of = [array for n in early for array in operands[n]]
    part = call(
        first_kernel, "virtual_first", like((share, columns), jnp.float32), [VMEM] * len(operands_of), 10**9
    )(*operands_of)
    last = call(
        last_kernel,
        "virtual_last",
        [like((share // 2, columns), jnp.float32)] * 2,
        [VMEM] * (1 + len(operands[late])),
        0,
        [pltpu.VMEM((share, columns), jnp.float32)],
    )
    stays, leaves = last(part, *operands[late])
    return (stays + send(leaves, 0, 1))[None]


def solution(mesh):
    in_specs = (
        P(("grid", "rep"), None),
        P(None, "grid"),
        P(("grid", "rep"), None),
        P("grid", "rep", None, None),
    )
    out_specs = P("grid", "rep", None)
    return jax.shard_map(shards, mesh=mesh, in_specs=in_specs, out_specs=out_specs, check_vma=False)
```

```python
import jax
import jax.numpy as jnp
from jax import lax
from jax.experimental import pallas as pl
from jax.experimental.pallas import tpu as pltpu
from jax.sharding import PartitionSpec as P

AXES = ("grid", "rep")
KERNEL_VMEM = 16 << 20
SQUARE = 4
CHUNK = 2
VMEM = pl.BlockSpec(memory_space=pltpu.VMEM)
ANY = pl.BlockSpec(memory_space=pl.ANY)


def position():
    rep = lax.axis_index("rep")
    return lax.axis_index("grid"), rep // 2, rep % 2


def half_kernel(green, half_green):
    half = half_green.shape[0]
    half_green[...] = green[pl.ds(pl.multiple_of(position()[2] * half, half), half), :]


def hold_kernel(array, after, held):
    held[...] = array[...]


def join_kernel(own, *rest):
    *halves, panels = rest
    half = halves[0].shape[0]
    core = position()[2]
    panels[len(halves) // 2] = own[...]
    for n in range(len(halves) // 2):
        for h, array in enumerate(halves[2 * n : 2 * n + 2]):
            start = pl.multiple_of((core ^ h) * half, half)
            panels[n, pl.ds(start, half), :] = array[...]


def source_of(array, start, size, rows, tail=None):
    labels = size - CHUNK * rows
    if tail is not None:
        labels = array.shape[0] - (CHUNK - 1) * rows
    tiles = [(array, start + labels + n * rows) for n in range(CHUNK)]
    if tail is not None:
        tiles[-1] = (tail, 0)
    return (array, start, labels), tiles


def add_products(picks, panel, green, sources, sums):
    wanted, width, rows = panel.astype(jnp.float32), green.shape[1], sums[0].shape[0]
    result = list(sums)
    for (array, start, labels), tiles in sources:
        names = array[start : start + labels, :width].astype(jnp.float32)
        for n, (tile, at) in enumerate(tiles):
            named = (names[n * picks : (n + 1) * picks] == wanted).astype(jnp.float32)
            product = jnp.dot(tile[at : at + rows, :], green, preferred_element_type=jnp.float32)
            product = (product * jnp.max(named, axis=0, keepdims=True)).astype(jnp.bfloat16)
            result[n] = result[n] + product.astype(jnp.float32)
    return result


def sums_kernel(picks, fars, chunk, split, own, first, second, corner, *rest):
    tail, rest = (rest[0], rest[1:]) if split else (None, rest)
    panels, after, *messages, total = rest
    pairs = len(messages) // len(fars)
    share = messages[0].shape[0] // CHUNK
    rows, width, size = share * pairs, panels.shape[2], own.shape[0]
    place, x, _ = position()
    starts = [(own, 0), (first, chunk * size), (second, 0)]
    every = [source_of(array, start, size, rows) for array, start in starts]
    every.append(source_of(corner, 0, size, rows, tail))
    for p, far in enumerate(fars):
        sums = [jnp.zeros((rows, width), jnp.float32)] * CHUNK
        for n, one in enumerate(add_products(picks, place ^ far, panels[p], every, sums)):
            total[n] = one
        for t in range(pairs):
            start = pl.multiple_of((x ^ t) * share, share)
            for n in range(CHUNK):
                block = total[n, pl.ds(start, share), :]
                message = messages[p * pairs + t]
                message[n * share : (n + 1) * share, :] = block.astype(message.dtype)


def virtual_sum(rows, operands):
    result = None
    for message, virtual in zip(operands[::2], operands[1::2]):
        for n in range(CHUNK):
            tile = message[n * rows : (n + 1) * rows, :]
            product = jnp.dot(tile, virtual[n], preferred_element_type=jnp.float32)
            result = product if result is None else result + product
    return result


def first_kernel(*refs):
    *operands, total = refs
    total[...] = virtual_sum(total.shape[0], operands)


def last_kernel(before, *refs):
    *operands, stays, leaves, total = refs
    middle = stays.shape[0]
    total[...] = before[...] + virtual_sum(total.shape[0], operands)
    core = position()[2]
    stays[...] = total[pl.ds(pl.multiple_of(core * middle, middle), middle), :]
    leaves[...] = total[pl.ds(pl.multiple_of((1 - core) * middle, middle), middle), :]


def call(kernel, name, out, specs, flops, scratch=()):
    def run(*operands):
        return pl.pallas_call(
            kernel,
            out_shape=out,
            in_specs=specs,
            out_specs=jax.tree.map(lambda _: VMEM, out),
            scratch_shapes=scratch,
            cost_estimate=pl.CostEstimate(flops=flops, bytes_accessed=0, transcendentals=0),
            compiler_params=pltpu.CompilerParams(vmem_limit_bytes=KERNEL_VMEM),
            name=name,
        )(*operands)

    return run


def shards(integrals, green_occ, tile_panels, virtual_blocks):
    grid_count, rep_count = lax.axis_size("grid"), lax.axis_size("rep")
    pairs = rep_count // 2
    tile_count, picks = tile_panels.shape
    rows, depth = integrals.shape[0] // tile_count, integrals.shape[1]
    width, columns = virtual_blocks.shape[-2:]
    share = rows // pairs

    def send(array, grid_bits, rep_bits=0):
        order = []
        for g in range(grid_count):
            for r in range(rep_count):
                order.append((g * rep_count + r, (g ^ grid_bits) * rep_count + (r ^ rep_bits)))
        return lax.ppermute(array, AXES, order)

    def like(shape, dtype):
        return jax.ShapeDtypeStruct(shape, dtype)

    label_rows = -(-CHUNK * picks // 16) * 16
    chunks = range(tile_count // CHUNK)
    size = label_rows + CHUNK * rows
    half = like((green_occ.shape[0] // 2, green_occ.shape[1]), green_occ.dtype)
    mine = call(half_kernel, "half", half, [VMEM], 0)(green_occ)
    blocks = integrals.reshape(len(chunks), CHUNK * rows, depth)
    named = tile_panels.reshape(len(chunks), CHUNK * picks, 1).astype(jnp.bfloat16)
    named = jnp.pad(named, ((0, 0), (0, label_rows - CHUNK * picks), (0, 0)), constant_values=-1)
    named = jnp.broadcast_to(named, (len(chunks), label_rows, depth))
    whole = jnp.concatenate([named, blocks], axis=1)
    own = [whole[n] for n in chunks]
    whole = whole.reshape(len(chunks) * size, depth)

    near = [n % 2 == 1 for n in chunks]
    first = send(whole, 1)
    second = {n: send(own[n], 2) for wanted in (True, False) for n in chunks if near[n] == wanted}
    fars = list(range(SQUARE, grid_count, SQUARE))
    kept = [send(mine, far) for far in fars]
    corner, cut = {}, size - rows
    for n in chunks:
        if near[n]:
            corner[n] = [send(second[n], 1)]
        else:
            corner[n] = [send(first[n * size : n * size + cut], 2), send(second[n][cut:], 1)]
    hold = call(hold_kernel, "hold", half, [VMEM, ANY], 0)
    halves = [array for one in kept for array in (one, send(hold(one, first), 0, 1))]
    fars = fars + [0]
    join = call(
        join_kernel,
        "join",
        like((len(fars),) + green_occ.shape, green_occ.dtype),
        [VMEM] * (1 + len(halves)),
        10**9,
    )
    panels = join(green_occ, *halves)

    virtual = [virtual_blocks[0]]
    virtual += [send(virtual[0], 0, 2 * t) for t in range(1, pairs)]
    virtual = [[array[n * CHUNK : (n + 1) * CHUNK] for n in chunks] for array in virtual]

    after, operands = mine, {}
    ordered = sorted(chunks, key=lambda n: not near[n])
    for n in ordered:
        outs = [like((CHUNK * share, width), jnp.bfloat16)] * (len(fars) * pairs)
        sums = call(
            lambda *refs, n=n: sums_kernel(picks, fars, n, not near[n], *refs),
            "sums",
            outs,
            [VMEM] * (4 + len(corner[n])) + [ANY],
            0,
            [pltpu.VMEM((CHUNK, rows, width), jnp.float32)],
        )
        parts = sums(own[n], first, second[n], *corner[n], panels, after)
        after = parts[0]
        operands[n] = []
        for p, far in enumerate(fars):
            for t in range(pairs):
                part = parts[p * pairs + t]
                message = send(part, far, 2 * t) if far or t else part
                operands[n] += [message, virtual[t][n]]

    *early, late = ordered
    operands_of = [array for n in early for array in operands[n]]
    part = call(
        first_kernel, "virtual_first", like((share, columns), jnp.float32), [VMEM] * len(operands_of), 10**9
    )(*operands_of)
    last = call(
        last_kernel,
        "virtual_last",
        [like((share // 2, columns), jnp.float32)] * 2,
        [VMEM] * (1 + len(operands[late])),
        0,
        [pltpu.VMEM((share, columns), jnp.float32)],
    )
    stays, leaves = last(part, *operands[late])
    return (stays + send(leaves, 0, 1))[None]


def solution(mesh):
    in_specs = (
        P(("grid", "rep"), None),
        P(None, "grid"),
        P(("grid", "rep"), None),
        P("grid", "rep", None, None),
    )
    out_specs = P("grid", "rep", None)
    return jax.shard_map(shards, mesh=mesh, in_specs=in_specs, out_specs=out_specs, check_vma=False)
```

```python
import jax
import jax.numpy as jnp
from jax import lax
from jax.experimental import pallas as pl
from jax.experimental.pallas import tpu as pltpu
from jax.sharding import PartitionSpec as P

AXES = ("grid", "rep")
KERNEL_VMEM = 16 << 20
SQUARE = 4
CHUNK = 2
VMEM = pl.BlockSpec(memory_space=pltpu.VMEM)
ANY = pl.BlockSpec(memory_space=pl.ANY)


def position():
    rep = lax.axis_index("rep")
    return lax.axis_index("grid"), rep // 2, rep % 2


def half_kernel(green, half_green):
    half = half_green.shape[0]
    half_green[...] = green[pl.ds(pl.multiple_of(position()[2] * half, half), half), :]


def hold_kernel(array, after, held):
    held[...] = array[...]


def join_kernel(own, *rest):
    *halves, panels = rest
    half = halves[0].shape[0]
    core = position()[2]
    panels[len(halves) // 2] = own[...]
    for n in range(len(halves) // 2):
        for h, array in enumerate(halves[2 * n : 2 * n + 2]):
            start = pl.multiple_of((core ^ h) * half, half)
            panels[n, pl.ds(start, half), :] = array[...]


def source_of(array, start, size, rows, tail=None):
    labels = size - CHUNK * rows
    if tail is not None:
        labels = array.shape[0] - (CHUNK - 1) * rows
    tiles = [(array, start + labels + n * rows) for n in range(CHUNK)]
    if tail is not None:
        tiles[-1] = (tail, 0)
    return (array, start, labels), tiles


def add_products(picks, panel, green, sources, sums):
    wanted, width, rows = panel.astype(jnp.float32), green.shape[1], sums[0].shape[0]
    result = list(sums)
    for (array, start, labels), tiles in sources:
        names = array[start : start + labels, :width].astype(jnp.float32)
        for n, (tile, at) in enumerate(tiles):
            named = (names[n * picks : (n + 1) * picks] == wanted).astype(jnp.float32)
            product = jnp.dot(tile[at : at + rows, :], green, preferred_element_type=jnp.float32)
            product = (product * jnp.max(named, axis=0, keepdims=True)).astype(jnp.bfloat16)
            result[n] = result[n] + product.astype(jnp.float32)
    return result


def sums_kernel(picks, fars, chunk, split, own, first, second, corner, *rest):
    tail, rest = (rest[0], rest[1:]) if split else (None, rest)
    panels, after, *messages, total = rest
    pairs = len(messages) // len(fars)
    share = messages[0].shape[0] // CHUNK
    rows, width, size = share * pairs, panels.shape[2], own.shape[0]
    place, x, _ = position()
    starts = [(own, 0), (first, chunk * size), (second, 0)]
    every = [source_of(array, start, size, rows) for array, start in starts]
    every.append(source_of(corner, 0, size, rows, tail))
    for p, far in enumerate(fars):
        sums = [jnp.zeros((rows, width), jnp.float32)] * CHUNK
        for n, one in enumerate(add_products(picks, place ^ far, panels[p], every, sums)):
            total[n] = one
        for t in range(pairs):
            start = pl.multiple_of((x ^ t) * share, share)
            for n in range(CHUNK):
                block = total[n, pl.ds(start, share), :]
                message = messages[p * pairs + t]
                message[n * share : (n + 1) * share, :] = block.astype(message.dtype)


def virtual_sum(rows, operands):
    result = None
    for message, virtual in zip(operands[::2], operands[1::2]):
        for n in range(CHUNK):
            tile = message[n * rows : (n + 1) * rows, :]
            product = jnp.dot(tile, virtual[n], preferred_element_type=jnp.float32)
            result = product if result is None else result + product
    return result


def first_kernel(*refs):
    *operands, total = refs
    total[...] = virtual_sum(total.shape[0], operands)


def last_kernel(before, *refs):
    *operands, stays, leaves, total = refs
    middle = stays.shape[0]
    total[...] = before[...] + virtual_sum(total.shape[0], operands)
    core = position()[2]
    stays[...] = total[pl.ds(pl.multiple_of(core * middle, middle), middle), :]
    leaves[...] = total[pl.ds(pl.multiple_of((1 - core) * middle, middle), middle), :]


def call(kernel, name, out, specs, flops, scratch=()):
    def run(*operands):
        return pl.pallas_call(
            kernel,
            out_shape=out,
            in_specs=specs,
            out_specs=jax.tree.map(lambda _: VMEM, out),
            scratch_shapes=scratch,
            cost_estimate=pl.CostEstimate(flops=flops, bytes_accessed=0, transcendentals=0),
            compiler_params=pltpu.CompilerParams(vmem_limit_bytes=KERNEL_VMEM),
            name=name,
        )(*operands)

    return run


def shards(integrals, green_occ, tile_panels, virtual_blocks):
    grid_count, rep_count = lax.axis_size("grid"), lax.axis_size("rep")
    pairs = rep_count // 2
    tile_count, picks = tile_panels.shape
    rows, depth = integrals.shape[0] // tile_count, integrals.shape[1]
    width, columns = virtual_blocks.shape[-2:]
    share = rows // pairs

    def send(array, grid_bits, rep_bits=0):
        order = []
        for g in range(grid_count):
            for r in range(rep_count):
                order.append((g * rep_count + r, (g ^ grid_bits) * rep_count + (r ^ rep_bits)))
        return lax.ppermute(array, AXES, order)

    def like(shape, dtype):
        return jax.ShapeDtypeStruct(shape, dtype)

    label_rows = -(-CHUNK * picks // 16) * 16
    chunks = range(tile_count // CHUNK)
    size = label_rows + CHUNK * rows
    half = like((green_occ.shape[0] // 2, green_occ.shape[1]), green_occ.dtype)
    mine = call(half_kernel, "half", half, [VMEM], 0)(green_occ)
    blocks = integrals.reshape(len(chunks), CHUNK * rows, depth)
    named = tile_panels.reshape(len(chunks), CHUNK * picks, 1).astype(jnp.bfloat16)
    named = jnp.pad(named, ((0, 0), (0, label_rows - CHUNK * picks), (0, 0)), constant_values=-1)
    named = jnp.broadcast_to(named, (len(chunks), label_rows, depth))
    whole = jnp.concatenate([named, blocks], axis=1)
    own = [whole[n] for n in chunks]
    whole = whole.reshape(len(chunks) * size, depth)

    near = [n % 2 == 1 for n in chunks]
    first = send(whole, 1)
    second = {n: send(own[n], 2) for wanted in (True, False) for n in chunks if near[n] == wanted}
    fars = list(range(SQUARE, grid_count, SQUARE))
    kept = [send(mine, far) for far in fars]
    corner, cut = {}, size - rows
    for n in chunks:
        if near[n]:
            corner[n] = [send(second[n], 1)]
        else:
            corner[n] = [send(first[n * size : n * size + cut], 2), send(second[n][cut:], 1)]
    hold = call(hold_kernel, "hold", half, [VMEM, ANY], 0)
    halves = [array for one in kept for array in (one, send(hold(one, first), 0, 1))]
    fars = fars + [0]
    join = call(
        join_kernel,
        "join",
        like((len(fars),) + green_occ.shape, green_occ.dtype),
        [VMEM] * (1 + len(halves)),
        10**9,
    )
    panels = join(green_occ, *halves)

    virtual = [virtual_blocks[0]]
    virtual += [send(virtual[0], 0, 2 * t) for t in range(1, pairs)]
    virtual = [[array[n * CHUNK : (n + 1) * CHUNK] for n in chunks] for array in virtual]

    after, operands = mine, {}
    ordered = sorted(chunks, key=lambda n: not near[n])
    for n in ordered:
        outs = [like((CHUNK * share, width), jnp.bfloat16)] * (len(fars) * pairs)
        sums = call(
            lambda *refs, n=n: sums_kernel(picks, fars, n, not near[n], *refs),
            "sums",
            outs,
            [VMEM] * (4 + len(corner[n])) + [ANY],
            0,
            [pltpu.VMEM((CHUNK, rows, width), jnp.float32)],
        )
        parts = sums(own[n], first, second[n], *corner[n], panels, after)
        after = parts[0]
        operands[n] = []
        for p, far in enumerate(fars):
            for t in reversed(range(pairs)):
                part = parts[p * pairs + t]
                message = send(part, far, 2 * t) if far or t else part
                operands[n] += [message, virtual[t][n]]

    *early, late = ordered
    operands_of = [array for n in early for array in operands[n]]
    part = call(
        first_kernel, "virtual_first", like((share, columns), jnp.float32), [VMEM] * len(operands_of), 10**9
    )(*operands_of)
    last = call(
        last_kernel,
        "virtual_last",
        [like((share // 2, columns), jnp.float32)] * 2,
        [VMEM] * (1 + len(operands[late])),
        0,
        [pltpu.VMEM((share, columns), jnp.float32)],
    )
    stays, leaves = last(part, *operands[late])
    return (stays + send(leaves, 0, 1))[None]


def solution(mesh):
    in_specs = (
        P(("grid", "rep"), None),
        P(None, "grid"),
        P(("grid", "rep"), None),
        P("grid", "rep", None, None),
    )
    out_specs = P("grid", "rep", None)
    return jax.shard_map(shards, mesh=mesh, in_specs=in_specs, out_specs=out_specs, check_vma=False)
```

```python
import jax
import jax.numpy as jnp
from jax import lax
from jax.experimental import pallas as pl
from jax.experimental.pallas import tpu as pltpu
from jax.sharding import PartitionSpec as P

AXES = ("grid", "rep")
KERNEL_VMEM = 16 << 20
SQUARE = 4
CHUNK = 2
SOON, FIRST = 10**9, 10**10
VMEM = pl.BlockSpec(memory_space=pltpu.VMEM)
ANY = pl.BlockSpec(memory_space=pl.ANY)


def position():
    rep = lax.axis_index("rep")
    return lax.axis_index("grid"), rep // 2, rep % 2


def half_kernel(green, half_green):
    half = half_green.shape[0]
    half_green[...] = green[pl.ds(pl.multiple_of(position()[2] * half, half), half), :]


def hold_kernel(array, after, held):
    held[...] = array[...]


def join_kernel(own, *rest):
    *halves, panels = rest
    half = halves[0].shape[0]
    core = position()[2]
    panels[len(halves) // 2] = own[...]
    for n in range(len(halves) // 2):
        for h, array in enumerate(halves[2 * n : 2 * n + 2]):
            start = pl.multiple_of((core ^ h) * half, half)
            panels[n, pl.ds(start, half), :] = array[...]


def source_of(array, start, size, rows, tail=None):
    labels = size - CHUNK * rows
    if tail is not None:
        labels = array.shape[0] - (CHUNK - 1) * rows
    tiles = [(array, start + labels + n * rows) for n in range(CHUNK)]
    if tail is not None:
        tiles[-1] = (tail, 0)
    return (array, start, labels), tiles


def add_products(picks, panel, green, sources, sums):
    wanted, width, rows = panel.astype(jnp.float32), green.shape[1], sums[0].shape[0]
    result = list(sums)
    for (array, start, labels), tiles in sources:
        names = array[start : start + labels, :width].astype(jnp.float32)
        for n, (tile, at) in enumerate(tiles):
            named = (names[n * picks : (n + 1) * picks] == wanted).astype(jnp.float32)
            product = jnp.dot(tile[at : at + rows, :], green, preferred_element_type=jnp.float32)
            product = (product * jnp.max(named, axis=0, keepdims=True)).astype(jnp.bfloat16)
            result[n] = result[n] + product.astype(jnp.float32)
    return result


def sums_kernel(picks, fars, chunk, split, own, first, second, corner, *rest):
    tail, rest = (rest[0], rest[1:]) if split else (None, rest)
    panels, after, *messages, total = rest
    rows, width, size = total.shape[1], panels.shape[2], own.shape[0]
    place, x, _ = position()
    starts = [(own, 0), (first, chunk * size), (second, 0)]
    sources = [source_of(array, start, size, rows) for array, start in starts]
    sources.append(source_of(corner, 0, size, rows, tail))
    zeros = [jnp.zeros((rows, width), jnp.float32)] * CHUNK
    at = 0
    for p, far in enumerate(fars):
        sums = add_products(picks, place ^ far, panels[p], sources, zeros)
        if not far:
            for n, one in enumerate(sums):
                messages[at][n * rows : (n + 1) * rows, :] = one.astype(messages[at].dtype)
            at += 1
            continue
        for n, one in enumerate(sums):
            total[n] = one
        share = messages[at].shape[0] // CHUNK
        for t in range(rows // share):
            start = pl.multiple_of((x ^ t) * share, share)
            for n in range(CHUNK):
                block = total[n, pl.ds(start, share), :]
                messages[at][n * share : (n + 1) * share, :] = block.astype(messages[at].dtype)
            at += 1


def virtual_sum(rows, operands):
    result = None
    for message, virtual in zip(operands[::2], operands[1::2]):
        for n in range(CHUNK):
            tile = message[n * rows : (n + 1) * rows, :]
            product = jnp.dot(tile, virtual[n], preferred_element_type=jnp.float32)
            result = product if result is None else result + product
    return result


def whole_kernel(count, *refs):
    operands, pieces, total = refs[:count], refs[count:-1], refs[-1]
    total[...] = virtual_sum(total.shape[0], operands)
    share = pieces[0].shape[0]
    x = position()[1]
    for t, piece in enumerate(pieces):
        piece[...] = total[pl.ds(pl.multiple_of((x ^ t) * share, share), share), :]


def far_kernel(*refs):
    *operands, total = refs
    total[...] = virtual_sum(total.shape[0], operands)


def split_kernel(*refs):
    *parts, stays, leaves, total = refs
    middle = stays.shape[0]
    total[...] = sum(part[...] for part in parts)
    core = position()[2]
    stays[...] = total[pl.ds(pl.multiple_of(core * middle, middle), middle), :]
    leaves[...] = total[pl.ds(pl.multiple_of((1 - core) * middle, middle), middle), :]


def call(kernel, name, out, specs, flops, scratch=()):
    def run(*operands):
        return pl.pallas_call(
            kernel,
            out_shape=out,
            in_specs=specs,
            out_specs=jax.tree.map(lambda _: VMEM, out),
            scratch_shapes=scratch,
            cost_estimate=pl.CostEstimate(flops=flops, bytes_accessed=0, transcendentals=0),
            compiler_params=pltpu.CompilerParams(vmem_limit_bytes=KERNEL_VMEM),
            name=name,
        )(*operands)

    return run


def shards(integrals, green_occ, tile_panels, virtual_blocks):
    grid_count, rep_count = lax.axis_size("grid"), lax.axis_size("rep")
    pairs = rep_count // 2
    tile_count, picks = tile_panels.shape
    rows, depth = integrals.shape[0] // tile_count, integrals.shape[1]
    width, columns = virtual_blocks.shape[-2:]
    share = rows // pairs

    def send(array, grid_bits, rep_bits=0):
        order = []
        for g in range(grid_count):
            for r in range(rep_count):
                order.append((g * rep_count + r, (g ^ grid_bits) * rep_count + (r ^ rep_bits)))
        return lax.ppermute(array, AXES, order)

    def like(shape, dtype):
        return jax.ShapeDtypeStruct(shape, dtype)

    label_rows = -(-CHUNK * picks // 16) * 16
    chunks = range(tile_count // CHUNK)
    size = label_rows + CHUNK * rows
    half = like((green_occ.shape[0] // 2, green_occ.shape[1]), green_occ.dtype)
    mine = call(half_kernel, "half", half, [VMEM], 0)(green_occ)
    blocks = integrals.reshape(len(chunks), CHUNK * rows, depth)
    named = tile_panels.reshape(len(chunks), CHUNK * picks, 1).astype(jnp.bfloat16)
    named = jnp.pad(named, ((0, 0), (0, label_rows - CHUNK * picks), (0, 0)), constant_values=-1)
    named = jnp.broadcast_to(named, (len(chunks), label_rows, depth))
    whole = jnp.concatenate([named, blocks], axis=1)
    own = [whole[n] for n in chunks]
    whole = whole.reshape(len(chunks) * size, depth)

    near = [n % 2 == 1 for n in chunks]
    first = send(whole, 1)
    second = {n: send(own[n], 2) for wanted in (True, False) for n in chunks if near[n] == wanted}
    fars = list(range(SQUARE, grid_count, SQUARE))
    kept = [send(mine, far) for far in fars]
    corner, cut = {}, size - rows
    for n in chunks:
        if near[n]:
            corner[n] = [send(second[n], 1)]
        else:
            corner[n] = [send(first[n * size : n * size + cut], 2), send(second[n][cut:], 1)]
    hold = call(hold_kernel, "hold", half, [VMEM, ANY], 0)
    halves = [array for one in kept for array in (one, send(hold(one, first), 0, 1))]
    fars = fars + [0]
    join = call(
        join_kernel,
        "join",
        like((len(fars),) + green_occ.shape, green_occ.dtype),
        [VMEM] * (1 + len(halves)),
        SOON,
    )
    panels = join(green_occ, *halves)

    blocks = [virtual_blocks[0, n * CHUNK : (n + 1) * CHUNK] for n in chunks]
    ordered = sorted(chunks, key=lambda n: not near[n])
    virtual = [virtual_blocks[0]]
    virtual += [send(virtual[0], 0, 2 * t) for t in range(1, pairs)]
    virtual = [[array[n * CHUNK : (n + 1) * CHUNK] for n in chunks] for array in virtual]

    after, own_operands, far_operands = mine, [], []
    for n in ordered:
        kept_rows, cut_rows = (like((CHUNK * size_of, width), jnp.bfloat16) for size_of in (rows, share))
        outs = []
        for far in fars:
            outs += [cut_rows] * pairs if far else [kept_rows]
        sums = call(
            lambda *refs, n=n: sums_kernel(picks, fars, n, not near[n], *refs),
            "sums",
            outs,
            [VMEM] * (4 + len(corner[n])) + [ANY],
            0,
            [pltpu.VMEM((CHUNK, rows, width), jnp.float32)],
        )
        parts = list(sums(own[n], first, second[n], *corner[n], panels, after))
        after = parts[0]
        far_operands.append([])
        for far in fars:
            if far:
                cut_parts, parts = parts[:pairs], parts[pairs:]
                for t in range(pairs):
                    far_operands[-1] += [send(cut_parts[t], far, 2 * t), virtual[t][n]]
            else:
                own_operands += [parts.pop(0), blocks[n]]

    piece = like((share, columns), jnp.float32)
    whole_product = call(
        lambda *refs: whole_kernel(len(own_operands), *refs),
        "virtual_own",
        [piece] * pairs,
        [VMEM] * len(own_operands),
        0,
        [pltpu.VMEM((rows, columns), jnp.float32)],
    )
    pieces = whole_product(*own_operands)
    pieces = [pieces[0]] + [send(pieces[t], 0, 2 * t) for t in range(1, pairs)]
    for each in far_operands:
        pieces.append(call(far_kernel, "virtual_far", piece, [VMEM] * len(each), FIRST)(*each))
    half_piece = like((share // 2, columns), jnp.float32)
    scratch = [pltpu.VMEM(piece.shape, piece.dtype)]
    split = call(split_kernel, "split", [half_piece] * 2, [VMEM] * len(pieces), 0, scratch)
    stays, leaves = split(*pieces)
    return (stays + send(leaves, 0, 1))[None]


def solution(mesh):
    in_specs = (
        P(("grid", "rep"), None),
        P(None, "grid"),
        P(("grid", "rep"), None),
        P("grid", "rep", None, None),
    )
    out_specs = P("grid", "rep", None)
    return jax.shard_map(shards, mesh=mesh, in_specs=in_specs, out_specs=out_specs, check_vma=False)
```

```python
import jax
import jax.numpy as jnp
from jax import lax
from jax.experimental import pallas as pl
from jax.experimental.pallas import tpu as pltpu
from jax.sharding import PartitionSpec as P

AXES = ("grid", "rep")
KERNEL_VMEM = 16 << 20
SQUARE = 4
CHUNK = 2
SOON, FIRST = 10**9, 10**10
VMEM = pl.BlockSpec(memory_space=pltpu.VMEM)
ANY = pl.BlockSpec(memory_space=pl.ANY)


def position():
    rep = lax.axis_index("rep")
    return lax.axis_index("grid"), rep // 2, rep % 2


def half_kernel(green, half_green):
    half = half_green.shape[0]
    half_green[...] = green[pl.ds(pl.multiple_of(position()[2] * half, half), half), :]


def hold_kernel(array, after, held):
    held[...] = array[...]


def join_kernel(own, *rest):
    *halves, panels = rest
    half = halves[0].shape[0]
    core = position()[2]
    panels[len(halves) // 2] = own[...]
    for n in range(len(halves) // 2):
        for h, array in enumerate(halves[2 * n : 2 * n + 2]):
            start = pl.multiple_of((core ^ h) * half, half)
            panels[n, pl.ds(start, half), :] = array[...]


def source_of(array, start, size, rows, tail=None):
    labels = size - CHUNK * rows
    if tail is not None:
        labels = array.shape[0] - (CHUNK - 1) * rows
    tiles = [(array, start + labels + n * rows) for n in range(CHUNK)]
    if tail is not None:
        tiles[-1] = (tail, 0)
    return (array, start, labels), tiles


def add_products(picks, panel, green, sources, sums):
    wanted, width, rows = panel.astype(jnp.float32), green.shape[1], sums[0].shape[0]
    result = list(sums)
    for (array, start, labels), tiles in sources:
        names = array[start : start + labels, :width].astype(jnp.float32)
        for n, (tile, at) in enumerate(tiles):
            named = (names[n * picks : (n + 1) * picks] == wanted).astype(jnp.float32)
            product = jnp.dot(tile[at : at + rows, :], green, preferred_element_type=jnp.float32)
            product = (product * jnp.max(named, axis=0, keepdims=True)).astype(jnp.bfloat16)
            result[n] = result[n] + product.astype(jnp.float32)
    return result


def sums_kernel(picks, fars, chunk, split, own, first, second, corner, *rest):
    tail, rest = (rest[0], rest[1:]) if split else (None, rest)
    panels, after, *messages, total = rest
    rows, width, size = total.shape[1], panels.shape[2], own.shape[0]
    place, x, _ = position()
    starts = [(own, 0), (first, chunk * size), (second, 0)]
    sources = [source_of(array, start, size, rows) for array, start in starts]
    sources.append(source_of(corner, 0, size, rows, tail))
    zeros = [jnp.zeros((rows, width), jnp.float32)] * CHUNK
    at = 0
    for p, far in enumerate(fars):
        sums = add_products(picks, place ^ far, panels[p], sources, zeros)
        if not far:
            for n, one in enumerate(sums):
                messages[at][n * rows : (n + 1) * rows, :] = one.astype(messages[at].dtype)
            at += 1
            continue
        for n, one in enumerate(sums):
            total[n] = one
        share = messages[at].shape[0] // CHUNK
        for t in range(rows // share):
            start = pl.multiple_of((x ^ t) * share, share)
            for n in range(CHUNK):
                block = total[n, pl.ds(start, share), :]
                messages[at][n * share : (n + 1) * share, :] = block.astype(messages[at].dtype)
            at += 1


def virtual_sum(rows, operands):
    result = None
    for message, virtual in zip(operands[::2], operands[1::2]):
        for n in range(CHUNK):
            tile = message[n * rows : (n + 1) * rows, :]
            product = jnp.dot(tile, virtual[n], preferred_element_type=jnp.float32)
            result = product if result is None else result + product
    return result


def whole_kernel(count, *refs):
    operands, pieces, total = refs[:count], refs[count + 1 : -1], refs[-1]
    total[...] = virtual_sum(total.shape[0], operands)
    share = pieces[0].shape[0]
    x = position()[1]
    for t, piece in enumerate(pieces):
        piece[...] = total[pl.ds(pl.multiple_of((x ^ t) * share, share), share), :]


def far_kernel(*refs):
    *operands, total = refs
    total[...] = virtual_sum(total.shape[0], operands)


def last_kernel(count, *refs):
    parts, (*operands, stays, leaves, total) = refs[:count], refs[count:]
    middle = stays.shape[0]
    total[...] = virtual_sum(total.shape[0], operands) + sum(part[...] for part in parts)
    core = position()[2]
    stays[...] = total[pl.ds(pl.multiple_of(core * middle, middle), middle), :]
    leaves[...] = total[pl.ds(pl.multiple_of((1 - core) * middle, middle), middle), :]


def call(kernel, name, out, specs, flops, scratch=()):
    def run(*operands):
        return pl.pallas_call(
            kernel,
            out_shape=out,
            in_specs=specs,
            out_specs=jax.tree.map(lambda _: VMEM, out),
            scratch_shapes=scratch,
            cost_estimate=pl.CostEstimate(flops=flops, bytes_accessed=0, transcendentals=0),
            compiler_params=pltpu.CompilerParams(vmem_limit_bytes=KERNEL_VMEM),
            name=name,
        )(*operands)

    return run


def shards(integrals, green_occ, tile_panels, virtual_blocks):
    grid_count, rep_count = lax.axis_size("grid"), lax.axis_size("rep")
    pairs = rep_count // 2
    tile_count, picks = tile_panels.shape
    rows, depth = integrals.shape[0] // tile_count, integrals.shape[1]
    width, columns = virtual_blocks.shape[-2:]
    share = rows // pairs

    def send(array, grid_bits, rep_bits=0):
        order = []
        for g in range(grid_count):
            for r in range(rep_count):
                order.append((g * rep_count + r, (g ^ grid_bits) * rep_count + (r ^ rep_bits)))
        return lax.ppermute(array, AXES, order)

    def like(shape, dtype):
        return jax.ShapeDtypeStruct(shape, dtype)

    label_rows = -(-CHUNK * picks // 16) * 16
    chunks = range(tile_count // CHUNK)
    size = label_rows + CHUNK * rows
    half = like((green_occ.shape[0] // 2, green_occ.shape[1]), green_occ.dtype)
    mine = call(half_kernel, "half", half, [VMEM], 0)(green_occ)
    blocks = integrals.reshape(len(chunks), CHUNK * rows, depth)
    named = tile_panels.reshape(len(chunks), CHUNK * picks, 1).astype(jnp.bfloat16)
    named = jnp.pad(named, ((0, 0), (0, label_rows - CHUNK * picks), (0, 0)), constant_values=-1)
    named = jnp.broadcast_to(named, (len(chunks), label_rows, depth))
    whole = jnp.concatenate([named, blocks], axis=1)
    own = [whole[n] for n in chunks]
    whole = whole.reshape(len(chunks) * size, depth)

    near = [n % 2 == 1 for n in chunks]
    first = send(whole, 1)
    second = {n: send(own[n], 2) for wanted in (True, False) for n in chunks if near[n] == wanted}
    fars = list(range(SQUARE, grid_count, SQUARE))
    kept = [send(mine, far) for far in fars]
    corner, cut = {}, size - rows
    for n in chunks:
        if near[n]:
            corner[n] = [send(second[n], 1)]
        else:
            corner[n] = [send(first[n * size : n * size + cut], 2), send(second[n][cut:], 1)]
    hold = call(hold_kernel, "hold", half, [VMEM, ANY], 0)
    halves = [array for one in kept for array in (one, send(hold(one, first), 0, 1))]
    fars = fars + [0]
    join = call(
        join_kernel,
        "join",
        like((len(fars),) + green_occ.shape, green_occ.dtype),
        [VMEM] * (1 + len(halves)),
        SOON,
    )
    panels = join(green_occ, *halves)

    blocks = [virtual_blocks[0, n * CHUNK : (n + 1) * CHUNK] for n in chunks]
    ordered = sorted(chunks, key=lambda n: not near[n])
    virtual = [virtual_blocks[0]]
    virtual += [send(virtual[0], 0, 2 * t) for t in range(1, pairs)]
    virtual = [[array[n * CHUNK : (n + 1) * CHUNK] for n in chunks] for array in virtual]

    after, own_operands, far_operands = mine, [], []
    for n in ordered:
        kept_rows, cut_rows = (like((CHUNK * size_of, width), jnp.bfloat16) for size_of in (rows, share))
        outs = []
        for far in fars:
            outs += [cut_rows] * pairs if far else [kept_rows]
        sums = call(
            lambda *refs, n=n: sums_kernel(picks, fars, n, not near[n], *refs),
            "sums",
            outs,
            [VMEM] * (4 + len(corner[n])) + [ANY],
            0,
            [pltpu.VMEM((CHUNK, rows, width), jnp.float32)],
        )
        parts = list(sums(own[n], first, second[n], *corner[n], panels, after))
        after = parts[0]
        far_operands.append([])
        for far in fars:
            if far:
                cut_parts, parts = parts[:pairs], parts[pairs:]
                for t in range(pairs):
                    far_operands[-1] += [send(cut_parts[t], far, 2 * t), virtual[t][n]]
            else:
                own_operands += [parts.pop(0), blocks[n]]

    piece = like((share, columns), jnp.float32)
    whole_product = call(
        lambda *refs: whole_kernel(len(own_operands), *refs),
        "virtual_own",
        [piece] * pairs,
        [VMEM] * len(own_operands) + [ANY],
        0,
        [pltpu.VMEM((rows, columns), jnp.float32)],
    )
    pieces = whole_product(*own_operands, far_operands[0][0])
    pieces = [pieces[0]] + [send(pieces[t], 0, 2 * t) for t in range(1, pairs)]
    *early_operands, late_operands = far_operands
    for each in early_operands:
        pieces.append(call(far_kernel, "virtual_far", piece, [VMEM] * len(each), FIRST)(*each))
    half_piece = like((share // 2, columns), jnp.float32)
    scratch = [pltpu.VMEM(piece.shape, piece.dtype)]
    count = len(pieces)
    last = call(
        lambda *refs: last_kernel(count, *refs),
        "virtual_last",
        [half_piece] * 2,
        [VMEM] * (count + len(late_operands)),
        FIRST,
        scratch,
    )
    stays, leaves = last(*pieces, *late_operands)
    return (stays + send(leaves, 0, 1))[None]


def solution(mesh):
    in_specs = (
        P(("grid", "rep"), None),
        P(None, "grid"),
        P(("grid", "rep"), None),
        P("grid", "rep", None, None),
    )
    out_specs = P("grid", "rep", None)
    return jax.shard_map(shards, mesh=mesh, in_specs=in_specs, out_specs=out_specs, check_vma=False)
```

```python
import jax
import jax.numpy as jnp
from jax import lax
from jax.experimental import pallas as pl
from jax.experimental.pallas import tpu as pltpu
from jax.sharding import PartitionSpec as P

AXES = ("grid", "rep")
KERNEL_VMEM = 16 << 20
SQUARE = 4
CHUNK = 2
SOON, FIRST = 10**9, 10**10
VMEM = pl.BlockSpec(memory_space=pltpu.VMEM)
ANY = pl.BlockSpec(memory_space=pl.ANY)


def position():
    rep = lax.axis_index("rep")
    return lax.axis_index("grid"), rep // 2, rep % 2


def half_kernel(green, half_green):
    half = half_green.shape[0]
    half_green[...] = green[pl.ds(pl.multiple_of(position()[2] * half, half), half), :]


def hold_kernel(array, after, held):
    held[...] = array[...]


def join_kernel(own, *rest):
    *halves, panels = rest
    half = halves[0].shape[0]
    core = position()[2]
    panels[len(halves) // 2] = own[...]
    for n in range(len(halves) // 2):
        for h, array in enumerate(halves[2 * n : 2 * n + 2]):
            start = pl.multiple_of((core ^ h) * half, half)
            panels[n, pl.ds(start, half), :] = array[...]


def source_of(array, start, size, rows, tail=None):
    labels = size - CHUNK * rows
    if tail is not None:
        labels = array.shape[0] - (CHUNK - 1) * rows
    tiles = [(array, start + labels + n * rows) for n in range(CHUNK)]
    if tail is not None:
        tiles[-1] = (tail, 0)
    return (array, start, labels), tiles


def add_products(picks, panel, green, sources, sums):
    wanted, width, rows = panel.astype(jnp.float32), green.shape[1], sums[0].shape[0]
    result = list(sums)
    for (array, start, labels), tiles in sources:
        names = array[start : start + labels, :width].astype(jnp.float32)
        for n, (tile, at) in enumerate(tiles):
            named = (names[n * picks : (n + 1) * picks] == wanted).astype(jnp.float32)
            product = jnp.dot(tile[at : at + rows, :], green, preferred_element_type=jnp.float32)
            product = (product * jnp.max(named, axis=0, keepdims=True)).astype(jnp.bfloat16)
            result[n] = result[n] + product.astype(jnp.float32)
    return result


def sums_kernel(picks, fars, chunk, split, own, first, second, corner, *rest):
    tail, rest = (rest[0], rest[1:]) if split else (None, rest)
    panels, after, *messages, total = rest
    rows, width, size = total.shape[1], panels.shape[2], own.shape[0]
    place, x, _ = position()
    starts = [(own, 0), (first, chunk * size), (second, 0)]
    sources = [source_of(array, start, size, rows) for array, start in starts]
    sources.append(source_of(corner, 0, size, rows, tail))
    zeros = [jnp.zeros((rows, width), jnp.float32)] * CHUNK
    at = 0
    for p, far in enumerate(fars):
        sums = add_products(picks, place ^ far, panels[p], sources, zeros)
        if not far:
            for n, one in enumerate(sums):
                messages[at][n * rows : (n + 1) * rows, :] = one.astype(messages[at].dtype)
            at += 1
            continue
        for n, one in enumerate(sums):
            total[n] = one
        share = messages[at].shape[0] // CHUNK
        for t in range(rows // share):
            start = pl.multiple_of((x ^ t) * share, share)
            for n in range(CHUNK):
                block = total[n, pl.ds(start, share), :]
                messages[at][n * share : (n + 1) * share, :] = block.astype(messages[at].dtype)
            at += 1


def virtual_sum(rows, operands):
    result = None
    for message, virtual in zip(operands[::2], operands[1::2]):
        for n in range(CHUNK):
            tile = message[n * rows : (n + 1) * rows, :]
            product = jnp.dot(tile, virtual[n], preferred_element_type=jnp.float32)
            result = product if result is None else result + product
    return result


def whole_kernel(count, *refs):
    operands, pieces, total = refs[:count], refs[count:-1], refs[-1]
    total[...] = virtual_sum(total.shape[0], operands)
    share = pieces[0].shape[0]
    x = position()[1]
    for t, piece in enumerate(pieces):
        piece[...] = total[pl.ds(pl.multiple_of((x ^ t) * share, share), share), :]


def far_kernel(*refs):
    *operands, total = refs
    total[...] = virtual_sum(total.shape[0], operands)


def split_kernel(*refs):
    *parts, stays, leaves, total = refs
    middle = stays.shape[0]
    total[...] = sum(part[...] for part in parts)
    core = position()[2]
    stays[...] = total[pl.ds(pl.multiple_of(core * middle, middle), middle), :]
    leaves[...] = total[pl.ds(pl.multiple_of((1 - core) * middle, middle), middle), :]


def add_kernel(kept, came, total):
    total[0] = kept[...] + came[...]


def call(kernel, name, out, specs, flops, scratch=()):
    def run(*operands):
        return pl.pallas_call(
            kernel,
            out_shape=out,
            in_specs=specs,
            out_specs=jax.tree.map(lambda _: VMEM, out),
            scratch_shapes=scratch,
            cost_estimate=pl.CostEstimate(flops=flops, bytes_accessed=0, transcendentals=0),
            compiler_params=pltpu.CompilerParams(vmem_limit_bytes=KERNEL_VMEM),
            name=name,
        )(*operands)

    return run


def shards(integrals, green_occ, tile_panels, virtual_blocks):
    grid_count, rep_count = lax.axis_size("grid"), lax.axis_size("rep")
    pairs = rep_count // 2
    tile_count, picks = tile_panels.shape
    rows, depth = integrals.shape[0] // tile_count, integrals.shape[1]
    width, columns = virtual_blocks.shape[-2:]
    share = rows // pairs

    def send(array, grid_bits, rep_bits=0):
        order = []
        for g in range(grid_count):
            for r in range(rep_count):
                order.append((g * rep_count + r, (g ^ grid_bits) * rep_count + (r ^ rep_bits)))
        return lax.ppermute(array, AXES, order)

    def like(shape, dtype):
        return jax.ShapeDtypeStruct(shape, dtype)

    label_rows = -(-CHUNK * picks // 16) * 16
    chunks = range(tile_count // CHUNK)
    size = label_rows + CHUNK * rows
    half = like((green_occ.shape[0] // 2, green_occ.shape[1]), green_occ.dtype)
    mine = call(half_kernel, "half", half, [VMEM], 0)(green_occ)
    blocks = integrals.reshape(len(chunks), CHUNK * rows, depth)
    named = tile_panels.reshape(len(chunks), CHUNK * picks, 1).astype(jnp.bfloat16)
    named = jnp.pad(named, ((0, 0), (0, label_rows - CHUNK * picks), (0, 0)), constant_values=-1)
    named = jnp.broadcast_to(named, (len(chunks), label_rows, depth))
    whole = jnp.concatenate([named, blocks], axis=1)
    own = [whole[n] for n in chunks]
    whole = whole.reshape(len(chunks) * size, depth)

    near = [n % 2 == 1 for n in chunks]
    first = send(whole, 1)
    second = {n: send(own[n], 2) for wanted in (True, False) for n in chunks if near[n] == wanted}
    fars = list(range(SQUARE, grid_count, SQUARE))
    kept = [send(mine, far) for far in fars]
    corner, cut = {}, size - rows
    for n in chunks:
        if near[n]:
            corner[n] = [send(second[n], 1)]
        else:
            corner[n] = [send(first[n * size : n * size + cut], 2), send(second[n][cut:], 1)]
    hold = call(hold_kernel, "hold", half, [VMEM, ANY], 0)
    halves = [array for one in kept for array in (one, send(hold(one, first), 0, 1))]
    fars = fars + [0]
    join = call(
        join_kernel,
        "join",
        like((len(fars),) + green_occ.shape, green_occ.dtype),
        [VMEM] * (1 + len(halves)),
        SOON,
    )
    panels = join(green_occ, *halves)

    blocks = [virtual_blocks[0, n * CHUNK : (n + 1) * CHUNK] for n in chunks]
    ordered = sorted(chunks, key=lambda n: not near[n])
    virtual = [virtual_blocks[0]]
    virtual += [send(virtual[0], 0, 2 * t) for t in range(1, pairs)]
    virtual = [[array[n * CHUNK : (n + 1) * CHUNK] for n in chunks] for array in virtual]

    after, own_operands, far_operands = mine, [], []
    for n in ordered:
        kept_rows, cut_rows = (like((CHUNK * size_of, width), jnp.bfloat16) for size_of in (rows, share))
        outs = []
        for far in fars:
            outs += [cut_rows] * pairs if far else [kept_rows]
        sums = call(
            lambda *refs, n=n: sums_kernel(picks, fars, n, not near[n], *refs),
            "sums",
            outs,
            [VMEM] * (4 + len(corner[n])) + [ANY],
            0,
            [pltpu.VMEM((CHUNK, rows, width), jnp.float32)],
        )
        parts = list(sums(own[n], first, second[n], *corner[n], panels, after))
        after = parts[0]
        far_operands.append([])
        for far in fars:
            if far:
                cut_parts, parts = parts[:pairs], parts[pairs:]
                for t in range(pairs):
                    far_operands[-1] += [send(cut_parts[t], far, 2 * t), virtual[t][n]]
            else:
                own_operands += [parts.pop(0), blocks[n]]

    piece = like((share, columns), jnp.float32)
    whole_product = call(
        lambda *refs: whole_kernel(len(own_operands), *refs),
        "virtual_own",
        [piece] * pairs,
        [VMEM] * len(own_operands),
        0,
        [pltpu.VMEM((rows, columns), jnp.float32)],
    )
    pieces = whole_product(*own_operands)
    pieces = [pieces[0]] + [send(pieces[t], 0, 2 * t) for t in range(1, pairs)]
    for each in far_operands:
        pieces.append(call(far_kernel, "virtual_far", piece, [VMEM] * len(each), FIRST)(*each))
    half_piece = like((share // 2, columns), jnp.float32)
    scratch = [pltpu.VMEM(piece.shape, piece.dtype)]
    split = call(split_kernel, "split", [half_piece] * 2, [VMEM] * len(pieces), 0, scratch)
    stays, leaves = split(*pieces)
    result = like((1,) + half_piece.shape, half_piece.dtype)
    return call(add_kernel, "add", result, [VMEM] * 2, 0)(stays, send(leaves, 0, 1))


def solution(mesh):
    in_specs = (
        P(("grid", "rep"), None),
        P(None, "grid"),
        P(("grid", "rep"), None),
        P("grid", "rep", None, None),
    )
    out_specs = P("grid", "rep", None)
    return jax.shard_map(shards, mesh=mesh, in_specs=in_specs, out_specs=out_specs, check_vma=False)
```
